32 devices in a mesh: rows: 16 (over z, x, core), lev: 2 (over y).
Axes of the slice: x: 2, y: 2, z: 4, core: 2. Of those that a mesh axis runs over, the one named last changes fastest.
Arguments:
- field: bfloat16 [2, 8, 256, 64, 1024], P(None, 'lev', 'rows'), may hold values from -6 to 6
- spectral_weight: bfloat16 [3, 64, 64, 64, 64], P(None, None, 'rows'), may hold values from -5 to 5
- local_weight: bfloat16 [64, 64], replicated, may hold values from -0.75 to 0.75
- local_bias: float32 [64], replicated, may hold values from -4 to 4
- gate_weight: bfloat16 [64, 256], replicated, may hold values from -0.75 to 0.75
- up_weight: bfloat16 [64, 256], replicated, may hold values from -0.75 to 0.75
- down_weight: bfloat16 [256, 64], replicated, may hold values from -0.375 to 0.375
Outputs:
- updated: bfloat16 [2, 8, 256, 64, 1024], P(None, 'lev', 'rows')
The draws below stay inside these ranges and needn't reach their ends.
All inputs are finite; a program needn't handle non-finite values.
Results may differ from the reference program's by a relative error of at most 0.02.
Values may be sent and summed in bfloat16 or wider, within the bound.
No kernel may reach another device: no remote copies, remote signals or barrier semaphores. Data moves between devices by JAX's collectives and lax.ppermute only.
A program may use at most 128 MiB of HBM per device.

```python
import math
import jax
import jax.numpy as jnp
from jax import lax

B = 2
LEV = 8
NLON = 1024
C = 64
HID = 256
KLAT = 64
KLON = 64
NLAT = 256


def shard_levels(stream_key, dims, split, least, largest):
    def one(axis_at, parts):
        heights = jax.random.uniform(jax.random.fold_in(jax.random.fold_in(stream_key, 6), axis_at), (parts,), jnp.float32, least / len(split), largest / len(split))
        return jnp.repeat(jnp.exp(heights), dims[axis_at] // parts).reshape((-1,) + (1,) * (len(dims) - axis_at - 1))

    loudness = one(*split[0])
    for cut in split[1:]:
        loudness = loudness * one(*cut)
    return loudness


def centred(key, dims, width, bound, split=(), kind=jnp.bfloat16):
    gain = shard_levels(key, dims, split, -0.22, 0.18) if split else 1.0
    array = jax.random.normal(key, dims, jnp.float32) * width * gain
    return jnp.minimum(jnp.maximum(array, -bound), bound).astype(kind)


def setup_inputs(seed: int = 0) -> dict:
    arg_keys = jax.random.split(jax.random.key(seed), 8)
    field = centred(arg_keys[0], (B, LEV, NLAT, C, NLON), 1.0, 6.0, ((1, 2), (2, 16)))
    spectral_weight = centred(arg_keys[1], (3, KLAT, KLON, C, C), 0.8, 5.0, ((2, 16),))
    local_weight = centred(arg_keys[2], (C, C), C ** -0.5, 0.75)
    local_bias = centred(arg_keys[3], (C,), 1.0, 4.0, (), jnp.float32)
    gate_weight = centred(arg_keys[4], (C, HID), C ** -0.5, 0.75)
    up_weight = centred(arg_keys[5], (C, HID), C ** -0.5, 0.75)
    down_weight = centred(arg_keys[6], (HID, C), HID ** -0.5, 0.375)
    return dict(field=field, spectral_weight=spectral_weight, local_weight=local_weight, local_bias=local_bias, gate_weight=gate_weight, up_weight=up_weight, down_weight=down_weight)


def cas_rows(positions, count, modes):
    freq = jnp.arange(modes, dtype=jnp.int32) - modes // 2
    turns = positions[:, None] * freq[None, :] % count
    angle = 2.0 * math.pi / count * turns.astype(jnp.float32)
    return (jnp.cos(angle) + jnp.sin(angle)) / math.sqrt(count)

def rounded(value):
    return lax.optimization_barrier(value.astype(jnp.bfloat16))

def reference(field, spectral_weight, local_weight, local_bias, gate_weight, up_weight, down_weight):
    high = lax.Precision.HIGHEST
    lon_table = cas_rows(jnp.arange(NLON, dtype=jnp.int32), NLON, KLON).astype(jnp.bfloat16)
    lat_table = cas_rows(jnp.arange(NLAT, dtype=jnp.int32), NLAT, KLAT)
    along = jnp.dot(field.reshape(-1, NLON), lon_table, preferred_element_type=jnp.float32)
    along = along.reshape(B, LEV, NLAT, C, KLON)
    modes = jnp.einsum('nk,blncm->blkcm', lat_table, along, precision=high)
    modes_b = rounded(modes).astype(jnp.float32)
    padded = jnp.pad(modes_b, ((0, 0), (1, 1), (0, 0), (0, 0), (0, 0)))
    mixed = jnp.zeros((B, LEV, KLAT, C, KLON), jnp.float32)
    for shift_level in range(3):
        mixed = mixed + jnp.einsum('kmco,blkcm->blkom', spectral_weight[shift_level].astype(jnp.float32), padded[:, shift_level:shift_level + LEV], precision=high)
    mixed_b = rounded(mixed).astype(jnp.float32)
    back = jnp.einsum('nk,blkom->blnom', lat_table, mixed_b, precision=high)
    back_b = rounded(back)
    local_f = local_weight.astype(jnp.float32)
    gate_f = gate_weight.astype(jnp.float32)
    up_f = up_weight.astype(jnp.float32)
    down_f = down_weight.astype(jnp.float32)

    def finish(pair):
        grid, coarse = pair
        spectral = jnp.dot(coarse.reshape(-1, KLON), lon_table.T, preferred_element_type=jnp.float32)
        spectral = spectral.reshape(NLAT, C, NLON)
        grid_f = grid.astype(jnp.float32)
        local = jnp.einsum('co,ncx->nox', local_f, grid_f, precision=high)
        value = spectral + local + local_bias[None, :, None]
        act = rounded(jax.nn.gelu(value, approximate=False)).astype(jnp.float32)
        gate = jnp.einsum('ch,ncx->nhx', gate_f, act, precision=high)
        upper = jnp.einsum('ch,ncx->nhx', up_f, act, precision=high)
        hidden = rounded(jax.nn.silu(gate) * upper).astype(jnp.float32)
        down = jnp.einsum('hc,nhx->ncx', down_f, hidden, precision=high)
        return (grid_f + down).astype(jnp.bfloat16)
    result = lax.map(finish, (field.reshape(B * LEV, NLAT, C, NLON), back_b.reshape(B * LEV, NLAT, C, KLON)))
    return result.reshape(B, LEV, NLAT, C, NLON)
```

```python
import functools
import math

import jax
import jax.numpy as jnp
import ml_dtypes
import numpy as np
from jax import lax
from jax.experimental import pallas as pl
from jax.experimental.pallas import tpu as pltpu
from jax.sharding import PartitionSpec as P

BF = jnp.bfloat16
F32 = jnp.float32
NT = (((1,), (1,)), ((), ()))


def cas_table(count, modes):
    turns = np.arange(count)[:, None] * (np.arange(modes)[None, :] - modes // 2) % count
    angle = 2.0 * math.pi / count * turns
    return ((np.cos(angle) + np.sin(angle)) / math.sqrt(count)).astype(np.float32)


def split(table):
    high = table.astype(ml_dtypes.bfloat16)
    low = (table - high.astype(np.float32)).astype(ml_dtypes.bfloat16)
    return high, low


def call(kernel, grid, in_specs, out_specs, out_shape, scratch, flops, moved, **kw):
    return pl.pallas_call(
        kernel,
        grid=grid,
        in_specs=in_specs,
        out_specs=out_specs,
        out_shape=out_shape,
        scratch_shapes=scratch,
        compiler_params=pltpu.CompilerParams(
            dimension_semantics=("arbitrary",) * len(grid), vmem_limit_bytes=48 * 2**20
        ),
        cost_estimate=pl.CostEstimate(flops=flops, bytes_accessed=moved, transcendentals=0),
        **kw,
    )


def lanes(rows, wide):
    return pltpu.VMEM((wide // 128, rows, 128), F32)


def every(ref, start, size, stride):
    return jnp.concatenate(
        [ref[p, pl.ds(start, size, stride=stride), :] for p in range(ref.shape[0])], axis=1
    )


def put(ref, at, value):
    for p in range(ref.shape[0]):
        ref[p, at, :] = value[:, p * 128 : (p + 1) * 128]


def whole(shape):
    return pl.BlockSpec(shape, lambda *_: (0,) * len(shape))


def forward_kernel(ranks, field_ref, lon_ref, out_ref, held):
    _, _, rows, chans, cells = field_ref.shape
    modes = lon_ref.shape[0]
    band = modes // ranks
    values = lax.dot_general(
        lon_ref[...], field_ref[0, 0].reshape(rows * chans, cells), NT, preferred_element_type=F32
    )
    for n in range(rows):
        piece = values[:, n * chans : (n + 1) * chans]
        row = jnp.concatenate([piece[j * ranks : (j + 1) * ranks] for j in range(band)], axis=1)
        put(held, pl.ds(n * ranks, ranks), row)
    for r in range(ranks):
        out_ref[r, 0] = every(held, r, rows, ranks).astype(BF)


def forward(field, lon_rows, batch_at, ranks):
    _, levels, rows, chans, cells = field.shape
    modes = lon_rows.shape[0]
    wide = modes // ranks * chans
    return call(
        functools.partial(forward_kernel, ranks),
        (levels,),
        [
            pl.BlockSpec((1, 1, rows, chans, cells), lambda l: (batch_at, l, 0, 0, 0)),
            whole((modes, cells)),
        ],
        pl.BlockSpec((ranks, 1, rows, wide), lambda l: (0, l, 0, 0)),
        jax.ShapeDtypeStruct((ranks, levels, rows, wide), BF),
        [lanes(rows * ranks, wide)],
        2 * levels * rows * chans * cells * modes,
        levels * rows * chans * cells * 2,
    )(field, lon_rows)


def modes_kernel(table_ref, along_ref, out_ref):
    ranks, levels, rows, wide = along_ref.shape
    count = out_ref.shape[1]
    for l in range(levels):
        both = jnp.dot(
            table_ref[...],
            along_ref[:, l].reshape(ranks * rows, wide),
            preferred_element_type=F32,
        )
        out_ref[l] = (both[:count] + both[count:]).astype(BF)


def to_modes(table, along):
    ranks, levels, rows, wide = along.shape
    count = table.shape[0] // 2
    return call(
        modes_kernel,
        (1,),
        [whole(table.shape), whole(along.shape)],
        whole((levels, count, wide)),
        jax.ShapeDtypeStruct((levels, count, wide), BF),
        [],
        2 * levels * 2 * count * ranks * rows * wide,
        along.size * 2,
    )(table, along)


def mix_kernel(
    levels, below_ref, modes_ref, above_ref, weight_ref, table_ref, out_ref, held, mixed
):
    lat_modes, band, chans = weight_ref.shape[1:4]
    ranks, _, rows, wide = out_ref.shape
    step = held.shape[1] // lat_modes

    for l in range(levels + 2):
        source = below_ref[0] if l == 0 else above_ref[0] if l > levels else modes_ref[l - 1]
        put(held, pl.ds(l, lat_modes, stride=step), source.astype(F32))

    def one(k, carry):
        at = pl.multiple_of(k * step, 8)
        tile = jnp.concatenate([held[p, pl.ds(at, step), :] for p in range(wide // 128)], axis=1)
        parts = []
        for j in range(band):
            lhs = jnp.concatenate(
                [tile[d : d + levels, j * chans : (j + 1) * chans] for d in range(3)], axis=1
            ).astype(BF)
            weight = weight_ref[:, k, j].reshape(3 * chans, chans)
            parts.append(jnp.dot(lhs, weight, preferred_element_type=F32))
        put(mixed, pl.ds(at, levels), jnp.concatenate(parts, axis=1))
        return carry

    lax.fori_loop(0, lat_modes, one, 0, unroll=4)
    for l in range(levels):
        value = every(mixed, l, lat_modes, step).astype(BF)
        back = jnp.dot(
            table_ref[...], jnp.concatenate([value, value], axis=0), preferred_element_type=F32
        )
        out_ref[:, l] = back.astype(BF).reshape(ranks, rows, wide)


def mix(below, modes, above, weight, table, ranks):
    levels, lat_modes, wide = modes.shape
    rows = table.shape[0] // ranks
    step = (levels + 2 + 7) // 8 * 8
    return call(
        functools.partial(mix_kernel, levels),
        (1,),
        [
            whole(below.shape),
            whole(modes.shape),
            whole(above.shape),
            whole(weight.shape),
            whole(table.shape),
        ],
        whole((ranks, levels, rows, wide)),
        jax.ShapeDtypeStruct((ranks, levels, rows, wide), BF),
        [lanes(lat_modes * step, wide), lanes(lat_modes * step, wide)],
        weight.size * 2 * levels,
        weight.size * 4,
    )(below, modes, above, weight, table)


def gelu(value):
    return 0.5 * value * (1.0 + lax.erf(value * math.sqrt(0.5)))


def finish_kernel(
    block, field_ref, back_ref, lon_ref, local_ref, bias_ref, into_ref, down_ref, *rest
):
    out_ref, held, coarse = rest[-3:]
    ranks, _, rows, wide = back_ref.shape
    chans, cells = field_ref.shape[3:]
    band = wide // chans
    hid = down_ref.shape[1]
    at = pl.program_id(1)

    @pl.when(at == 0)
    def _():
        put(held, slice(None), back_ref[:, 0].astype(F32).reshape(ranks * rows, wide))
        for n in range(rows):
            tile = every(held, n, ranks, rows)
            stacked = jnp.concatenate(
                [tile[:, j * chans : (j + 1) * chans] for j in range(band)], axis=0
            )
            coarse[n] = jnp.concatenate([stacked.T.astype(BF), local_ref[...]], axis=1)

    tile_x = min(256, cells)

    def one(i, carry):
        n = at * block + i
        lhs = coarse[n]
        for x in range(0, cells, tile_x):
            span = slice(x, x + tile_x)
            grid = field_ref[0, 0, i, :, span]
            value = jnp.dot(
                lhs,
                jnp.concatenate([lon_ref[:, span], grid], axis=0),
                preferred_element_type=F32,
            )
            act = gelu(value + bias_ref[...]).astype(BF)
            both = jnp.dot(into_ref[...], act, preferred_element_type=F32)
            half = both[:hid]
            hidden = ((half + half * jnp.tanh(half)) * both[hid:]).astype(BF)
            down = jnp.dot(down_ref[...], hidden, preferred_element_type=F32)
            out_ref[0, 0, i, :, span] = (grid.astype(F32) + down).astype(BF)
        return carry

    lax.fori_loop(0, block, one, 0)


def finish(field, back, lon_rows, local, bias, into, down, batch_at, earlier, block=4):
    batch, levels, rows, chans, cells = field.shape
    ranks, _, _, wide = back.shape
    modes = lon_rows.shape[0]
    block = math.gcd(block, rows)
    spot = pl.BlockSpec((1, 1, block, chans, cells), lambda l, n: (batch_at, l, n, 0, 0))
    operands = [field, back, lon_rows, local, bias, into, down]
    in_specs = [
        spot,
        pl.BlockSpec((ranks, 1, rows, wide), lambda l, n: (0, l, 0, 0)),
        whole(lon_rows.shape),
        whole(local.shape),
        whole(bias.shape),
        whole(into.shape),
        whole(down.shape),
    ]
    kw = {}
    if earlier is not None:
        operands.append(earlier)
        in_specs.append(pl.BlockSpec(memory_space=pl.ANY))
        kw["input_output_aliases"] = {7: 0}
    return call(
        functools.partial(finish_kernel, block),
        (levels, rows // block),
        in_specs,
        spot,
        jax.ShapeDtypeStruct(field.shape, BF),
        [
            lanes(ranks * rows, wide),
            pltpu.VMEM((rows, chans, modes + chans), BF),
        ],
        2 * levels * rows * cells * chans * (modes + chans + 3 * down.shape[1]),
        levels * rows * chans * cells * 4,
        **kw,
    )(*operands)


def body(field, spectral_weight, local_weight, local_bias, gate_weight, up_weight, down_weight):
    batch, levels, rows, chans, cells = field.shape
    ranks = lax.axis_size("rows")
    sides = lax.axis_size("lev")
    lat_modes = spectral_weight.shape[1]
    band = spectral_weight.shape[2]
    lon_modes = band * ranks
    lon_rows = cas_table(cells, lon_modes).astype(ml_dtypes.bfloat16).T
    lon_rows = lon_rows.reshape(ranks, band, cells).swapaxes(0, 1).reshape(lon_modes, cells)
    lon_rows = jnp.asarray(np.ascontiguousarray(lon_rows))
    high, low = split(cas_table(rows * ranks, lat_modes))
    gather_table = jnp.asarray(np.concatenate([high.T, low.T], axis=0))
    spread_table = jnp.asarray(np.concatenate([high, low], axis=1))

    into = jnp.concatenate([gate_weight * BF(0.5), up_weight], axis=1).T
    down = down_weight.T
    local = local_weight.T
    bias = jnp.broadcast_to(local_bias[:, None], (chans, min(256, cells)))

    backs = []
    for b in range(batch):
        along = forward(field, lon_rows, b, ranks)
        along = lax.all_to_all(along, "rows", 0, 0, tiled=True)
        modes = to_modes(gather_table, along)
        below = lax.ppermute(modes[levels - 1 :], "lev", [(i, i + 1) for i in range(sides - 1)])
        above = lax.ppermute(modes[:1], "lev", [(i + 1, i) for i in range(sides - 1)])
        back = mix(below, modes, above, spectral_weight, spread_table, ranks)
        backs.append(lax.all_to_all(back, "rows", 0, 0, tiled=True))
    result = None
    for b in range(batch):
        result = finish(field, backs[b], lon_rows, local, bias, into, down, b, result)
    return result


def solution(mesh):
    return jax.shard_map(
        body,
        mesh=mesh,
        in_specs=(
            P(None, "lev", "rows", None, None),
            P(None, None, "rows", None, None),
            P(),
            P(),
            P(),
            P(),
            P(),
        ),
        out_specs=P(None, "lev", "rows", None, None),
        check_vma=False,
    )
```

```python
import functools
import math

import jax
import jax.numpy as jnp
import ml_dtypes
import numpy as np
from jax import lax
from jax.experimental import pallas as pl
from jax.experimental.pallas import tpu as pltpu
from jax.sharding import PartitionSpec as P

BF = jnp.bfloat16
F32 = jnp.float32
NT = (((1,), (1,)), ((), ()))


def cas_table(count, modes):
    turns = np.arange(count)[:, None] * (np.arange(modes)[None, :] - modes // 2) % count
    angle = 2.0 * math.pi / count * turns
    return ((np.cos(angle) + np.sin(angle)) / math.sqrt(count)).astype(np.float32)


def split(table):
    high = table.astype(ml_dtypes.bfloat16)
    low = (table - high.astype(np.float32)).astype(ml_dtypes.bfloat16)
    return high, low


def call(kernel, grid, in_specs, out_specs, out_shape, scratch, flops, moved, **kw):
    return pl.pallas_call(
        kernel,
        grid=grid,
        in_specs=in_specs,
        out_specs=out_specs,
        out_shape=out_shape,
        scratch_shapes=scratch,
        compiler_params=pltpu.CompilerParams(
            dimension_semantics=("arbitrary",) * len(grid), vmem_limit_bytes=48 * 2**20
        ),
        cost_estimate=pl.CostEstimate(flops=flops, bytes_accessed=moved, transcendentals=0),
        **kw,
    )


def lanes(rows, wide):
    return pltpu.VMEM((wide // 128, rows, 128), F32)


def every(ref, start, size, stride):
    return jnp.concatenate(
        [ref[p, pl.ds(start, size, stride=stride), :] for p in range(ref.shape[0])], axis=1
    )


def put(ref, at, value):
    for p in range(ref.shape[0]):
        ref[p, at, :] = value[:, p * 128 : (p + 1) * 128]


def whole(shape):
    return pl.BlockSpec(shape, lambda *_: (0,) * len(shape))


def forward_kernel(ranks, field_ref, lon_ref, out_ref, held):
    _, _, rows, chans, cells = field_ref.shape
    modes = lon_ref.shape[0]
    band = modes // ranks
    values = lax.dot_general(
        lon_ref[...], field_ref[0, 0].reshape(rows * chans, cells), NT, preferred_element_type=F32
    )
    for n in range(rows):
        piece = values[:, n * chans : (n + 1) * chans]
        row = jnp.concatenate([piece[j * ranks : (j + 1) * ranks] for j in range(band)], axis=1)
        put(held, pl.ds(n * ranks, ranks), row)
    for r in range(ranks):
        out_ref[r, 0] = every(held, r, rows, ranks).astype(BF)


def forward(field, lon_rows, batch_at, ranks):
    _, levels, rows, chans, cells = field.shape
    modes = lon_rows.shape[0]
    wide = modes // ranks * chans
    return call(
        functools.partial(forward_kernel, ranks),
        (levels,),
        [
            pl.BlockSpec((1, 1, rows, chans, cells), lambda l: (batch_at, l, 0, 0, 0)),
            whole((modes, cells)),
        ],
        pl.BlockSpec((ranks, 1, rows, wide), lambda l: (0, l, 0, 0)),
        jax.ShapeDtypeStruct((ranks, levels, rows, wide), BF),
        [lanes(rows * ranks, wide)],
        2 * levels * rows * chans * cells * modes,
        levels * rows * chans * cells * 2,
    )(field, lon_rows)


def modes_kernel(table_ref, along_ref, out_ref):
    ranks, levels, rows, wide = along_ref.shape
    count = out_ref.shape[1]
    for l in range(levels):
        both = jnp.dot(
            table_ref[...],
            along_ref[:, l].reshape(ranks * rows, wide),
            preferred_element_type=F32,
        )
        out_ref[l] = (both[:count] + both[count:]).astype(BF)


def to_modes(table, along):
    ranks, levels, rows, wide = along.shape
    count = table.shape[0] // 2
    return call(
        modes_kernel,
        (1,),
        [whole(table.shape), whole(along.shape)],
        whole((levels, count, wide)),
        jax.ShapeDtypeStruct((levels, count, wide), BF),
        [],
        2 * levels * 2 * count * ranks * rows * wide,
        along.size * 2,
    )(table, along)


def arrange_kernel(weight_ref, out_ref):
    shifts, part, band, chans, _ = weight_ref.shape
    for k in range(part):
        for d in range(shifts):
            out_ref[k, d * chans : (d + 1) * chans, :] = jnp.concatenate(
                [weight_ref[d, k, j] for j in range(band)], axis=1
            )


def arrange(weight, part=8):
    shifts, lat_modes, band, chans, outs = weight.shape
    return call(
        arrange_kernel,
        (lat_modes // part,),
        [pl.BlockSpec((shifts, part, band, chans, outs), lambda k: (0, k, 0, 0, 0))],
        pl.BlockSpec((part, shifts * chans, band * outs), lambda k: (k, 0, 0)),
        jax.ShapeDtypeStruct((lat_modes, shifts * chans, band * outs), BF),
        [],
        weight.size,
        weight.size * 6,
    )(weight)


def mix_kernel(below_ref, modes_ref, above_ref, weight_ref, table_ref, out_ref, held, mixed):
    lat_modes, deep, wide = weight_ref.shape
    ranks, levels, rows, _ = out_ref.shape
    chans = deep // 3
    band = wide // chans
    step = mixed.shape[1] // lat_modes

    near = [below_ref[0].astype(F32)]
    near += [modes_ref[l].astype(F32) for l in range(levels)]
    near += [above_ref[0].astype(F32)]
    fill = [jnp.zeros((lat_modes, held.shape[0] * 128 - deep), F32)]
    for j in range(band):
        span = slice(j * chans, (j + 1) * chans)
        for l in range(levels):
            row = jnp.concatenate([near[l + d][:, span] for d in range(3)] + fill, axis=1)
            put(held, pl.ds(j * levels + l, lat_modes, stride=step), row)

    for k in range(lat_modes):
        at = slice(k * step, (k + 1) * step)
        lhs = jnp.concatenate([held[p, at, :] for p in range(held.shape[0])], axis=1)
        lhs = lhs[:, :deep].astype(BF)
        put(mixed, at, jnp.dot(lhs, weight_ref[k], preferred_element_type=F32))

    owner = lax.broadcasted_iota(jnp.int32, (lat_modes, wide), 1) // chans
    for l in range(levels):
        value = every(mixed, l, lat_modes, step)
        for j in range(1, band):
            value = jnp.where(owner == j, every(mixed, j * levels + l, lat_modes, step), value)
        value = value.astype(BF)
        back = jnp.dot(
            table_ref[...], jnp.concatenate([value, value], axis=0), preferred_element_type=F32
        )
        out_ref[:, l] = back.astype(BF).reshape(ranks, rows, wide)


def mix(below, modes, above, weight, table, ranks):
    levels, lat_modes, wide = modes.shape
    rows = table.shape[0] // ranks
    deep = weight.shape[1]
    step = (levels * wide * 3 // deep + 7) // 8 * 8
    return call(
        mix_kernel,
        (1,),
        [
            whole(below.shape),
            whole(modes.shape),
            whole(above.shape),
            whole(weight.shape),
            whole(table.shape),
        ],
        whole((ranks, levels, rows, wide)),
        jax.ShapeDtypeStruct((ranks, levels, rows, wide), BF),
        [lanes(lat_modes * step, (deep + 127) // 128 * 128), lanes(lat_modes * step, wide)],
        weight.size * 2 * levels,
        weight.size * 2,
    )(below, modes, above, weight, table)


def finish_kernel(
    ahead, field_ref, back_ref, lon_ref, local_ref, bias_ref, into_ref, down_ref, *rest
):
    out_ref, held, coarse, act, hidden = rest[-5:]
    ranks, _, rows, wide = back_ref.shape
    chans, cells = field_ref.shape[3:]
    band = wide // chans
    hid = down_ref.shape[1]
    tile = min(256, cells)
    spans = [slice(x, x + tile) for x in range(0, cells, tile)]

    put(held, slice(None), back_ref[:, 0].astype(F32).reshape(ranks * rows, wide))
    for n in range(rows):
        piece = every(held, n, ranks, rows)
        stacked = jnp.concatenate(
            [piece[:, j * chans : (j + 1) * chans] for j in range(band)], axis=0
        )
        coarse[n] = jnp.concatenate([stacked.T.astype(BF), local_ref[...]], axis=1)

    def first(n, span):
        cells_in = jnp.concatenate([lon_ref[:, span], field_ref[0, 0, n, :, span]], axis=0)
        return jnp.dot(coarse[n], cells_in, preferred_element_type=F32)

    def store_act(u, span, value):
        value = value + bias_ref[...]
        half = 0.5 * value
        act[u, :, span] = (half + half * lax.erf(value * math.sqrt(0.5))).astype(BF)

    def last(u, n, span):
        down = jnp.dot(down_ref[...], hidden[u, :, span], preferred_element_type=F32)
        out_ref[0, 0, n, :, span] = (field_ref[0, 0, n, :, span].astype(F32) + down).astype(BF)

    for u in range(ahead):
        for span in spans:
            store_act(u, span, first(u, span))

    def one(t, carry):
        for u in range(ahead):
            n = t * ahead + u
            for span in spans:
                both = jnp.dot(into_ref[...], act[u, :, span], preferred_element_type=F32)
                last(u, jnp.maximum(n - ahead, 0), span)
                value = first(jnp.minimum(n + ahead, rows - 1), span)
                half = both[:hid]
                hidden[u, :, span] = ((half + half * jnp.tanh(half)) * both[hid:]).astype(BF)
                store_act(u, span, value)
        return carry

    lax.fori_loop(0, rows // ahead, one, 0)
    for u in range(ahead):
        for span in spans:
            last(u, rows - ahead + u, span)


def finish(field, back, lon_rows, local, bias, into, down, batch_at, earlier, ahead=2):
    batch, levels, rows, chans, cells = field.shape
    ranks, _, _, wide = back.shape
    modes = lon_rows.shape[0]
    spot = pl.BlockSpec((1, 1, rows, chans, cells), lambda l: (batch_at, l, 0, 0, 0))
    operands = [field, back, lon_rows, local, bias, into, down]
    in_specs = [
        spot,
        pl.BlockSpec((ranks, 1, rows, wide), lambda l: (0, l, 0, 0)),
        whole(lon_rows.shape),
        whole(local.shape),
        whole(bias.shape),
        whole(into.shape),
        whole(down.shape),
    ]
    kw = {}
    if earlier is not None:
        operands.append(earlier)
        in_specs.append(pl.BlockSpec(memory_space=pl.ANY))
        kw["input_output_aliases"] = {7: 0}
    return call(
        functools.partial(finish_kernel, ahead),
        (levels,),
        in_specs,
        spot,
        jax.ShapeDtypeStruct(field.shape, BF),
        [
            lanes(ranks * rows, wide),
            pltpu.VMEM((rows, chans, modes + chans), BF),
            pltpu.VMEM((ahead, chans, cells), BF),
            pltpu.VMEM((ahead, down.shape[1], cells), BF),
        ],
        2 * levels * rows * cells * chans * (modes + chans + 3 * down.shape[1]),
        levels * rows * chans * cells * 4,
        **kw,
    )(*operands)


def neighbours(modes, sides):
    if sides == 2:
        lower = lax.axis_index("lev") == 0
        got = lax.ppermute(
            jnp.where(lower, modes[-1:], modes[:1]), "lev", [(0, 1), (1, 0)]
        )
        none = jnp.zeros_like(got)
        return jnp.where(lower, none, got), jnp.where(lower, got, none)
    below = lax.ppermute(modes[-1:], "lev", [(i, i + 1) for i in range(sides - 1)])
    above = lax.ppermute(modes[:1], "lev", [(i + 1, i) for i in range(sides - 1)])
    return below, above


def body(field, spectral_weight, local_weight, local_bias, gate_weight, up_weight, down_weight):
    batch, levels, rows, chans, cells = field.shape
    ranks = lax.axis_size("rows")
    sides = lax.axis_size("lev")
    lat_modes = spectral_weight.shape[1]
    band = spectral_weight.shape[2]
    lon_modes = band * ranks
    lon_rows = cas_table(cells, lon_modes).astype(ml_dtypes.bfloat16).T
    lon_rows = lon_rows.reshape(ranks, band, cells).swapaxes(0, 1).reshape(lon_modes, cells)
    lon_rows = jnp.asarray(np.ascontiguousarray(lon_rows))
    high, low = split(cas_table(rows * ranks, lat_modes))
    gather_table = jnp.asarray(np.concatenate([high.T, low.T], axis=0))
    spread_table = jnp.asarray(np.concatenate([high, low], axis=1))

    into = jnp.concatenate([gate_weight * BF(0.5), up_weight], axis=1).T
    down = down_weight.T
    local = local_weight.T
    bias = jnp.broadcast_to(local_bias[:, None], (chans, min(256, cells)))

    weight = arrange(spectral_weight)
    sent = [forward(field, lon_rows, b, ranks) for b in range(batch)]
    backs = []
    for b in range(batch):
        along = lax.all_to_all(sent[b], "rows", 0, 0, tiled=True)
        if b == 0:
            along, weight = lax.optimization_barrier((along, weight))
        modes = to_modes(gather_table, along)
        if b + 1 < batch:
            modes, sent[b + 1] = lax.optimization_barrier((modes, sent[b + 1]))
        below, above = neighbours(modes, sides)
        back = mix(below, modes, above, weight, spread_table, ranks)
        backs.append(lax.all_to_all(back, "rows", 0, 0, tiled=True))
    result = None
    for b in range(batch):
        result = finish(field, backs[b], lon_rows, local, bias, into, down, b, result)
    return result


def solution(mesh):
    return jax.shard_map(
        body,
        mesh=mesh,
        in_specs=(
            P(None, "lev", "rows", None, None),
            P(None, None, "rows", None, None),
            P(),
            P(),
            P(),
            P(),
            P(),
        ),
        out_specs=P(None, "lev", "rows", None, None),
        check_vma=False,
    )
```

```python
import functools
import math

import jax
import jax.numpy as jnp
import ml_dtypes
import numpy as np
from jax import lax
from jax.experimental import pallas as pl
from jax.experimental.pallas import tpu as pltpu
from jax.sharding import PartitionSpec as P

BF = jnp.bfloat16
F32 = jnp.float32
NT = (((1,), (1,)), ((), ()))


def cas_table(count, modes):
    turns = np.arange(count)[:, None] * (np.arange(modes)[None, :] - modes // 2) % count
    angle = 2.0 * math.pi / count * turns
    return ((np.cos(angle) + np.sin(angle)) / math.sqrt(count)).astype(np.float32)


def split(table):
    high = table.astype(ml_dtypes.bfloat16)
    low = (table - high.astype(np.float32)).astype(ml_dtypes.bfloat16)
    return high, low


def call(kernel, grid, in_specs, out_specs, out_shape, scratch, flops, moved, room=48, **kw):
    return pl.pallas_call(
        kernel,
        grid=grid,
        in_specs=in_specs,
        out_specs=out_specs,
        out_shape=out_shape,
        scratch_shapes=scratch,
        compiler_params=pltpu.CompilerParams(
            dimension_semantics=("arbitrary",) * len(grid), vmem_limit_bytes=room * 2**20
        ),
        cost_estimate=pl.CostEstimate(flops=flops, bytes_accessed=moved, transcendentals=0),
        **kw,
    )


def lanes(rows, wide):
    return pltpu.VMEM((wide // 128, rows, 128), F32)


def every(ref, start, size, stride):
    return jnp.concatenate(
        [ref[p, pl.ds(start, size, stride=stride), :] for p in range(ref.shape[0])], axis=1
    )


def put(ref, at, value):
    for p in range(ref.shape[0]):
        ref[p, at, :] = value[:, p * 128 : (p + 1) * 128]


def whole(shape):
    return pl.BlockSpec(shape, lambda *_: (0,) * len(shape))


def forward_kernel(ranks, field_ref, lon_ref, out_ref, held):
    _, _, rows, chans, cells = field_ref.shape
    modes = lon_ref.shape[0]
    band = modes // ranks
    values = lax.dot_general(
        lon_ref[...], field_ref[0, 0].reshape(rows * chans, cells), NT, preferred_element_type=F32
    )
    for n in range(rows):
        piece = values[:, n * chans : (n + 1) * chans]
        row = jnp.concatenate([piece[j * ranks : (j + 1) * ranks] for j in range(band)], axis=1)
        put(held, pl.ds(n * ranks, ranks), row)
    for r in range(ranks):
        out_ref[r, 0] = every(held, r, rows, ranks).astype(BF)


def forward(field, lon_rows, batch_at, ranks):
    _, levels, rows, chans, cells = field.shape
    modes = lon_rows.shape[0]
    wide = modes // ranks * chans
    return call(
        functools.partial(forward_kernel, ranks),
        (levels,),
        [
            pl.BlockSpec((1, 1, rows, chans, cells), lambda l: (batch_at, l, 0, 0, 0)),
            whole((modes, cells)),
        ],
        pl.BlockSpec((ranks, 1, rows, wide), lambda l: (0, l, 0, 0)),
        jax.ShapeDtypeStruct((ranks, levels, rows, wide), BF),
        [lanes(rows * ranks, wide)],
        2 * levels * rows * chans * cells * modes,
        levels * rows * chans * cells * 2,
        room=60,
    )(field, lon_rows)


def modes_kernel(table_ref, along_ref, out_ref):
    ranks, levels, rows, wide = along_ref.shape
    count = out_ref.shape[1]
    for l in range(levels):
        both = jnp.dot(
            table_ref[...],
            along_ref[:, l].reshape(ranks * rows, wide),
            preferred_element_type=F32,
        )
        out_ref[l] = (both[:count] + both[count:]).astype(BF)


def to_modes(table, along):
    ranks, levels, rows, wide = along.shape
    count = table.shape[0] // 2
    return call(
        modes_kernel,
        (1,),
        [whole(table.shape), whole(along.shape)],
        whole((levels, count, wide)),
        jax.ShapeDtypeStruct((levels, count, wide), BF),
        [],
        2 * levels * 2 * count * ranks * rows * wide,
        along.size * 2,
    )(table, along)


def arrange_kernel(weight_ref, out_ref):
    shifts, part, band, chans, _ = weight_ref.shape
    for k in range(part):
        for d in range(shifts):
            out_ref[k, d * chans : (d + 1) * chans, :] = jnp.concatenate(
                [weight_ref[d, k, j] for j in range(band)], axis=1
            )


def arrange(weight, part=32):
    shifts, lat_modes, band, chans, outs = weight.shape
    part = math.gcd(part, lat_modes)
    return call(
        arrange_kernel,
        (lat_modes // part,),
        [pl.BlockSpec((shifts, part, band, chans, outs), lambda k: (0, k, 0, 0, 0))],
        pl.BlockSpec((part, shifts * chans, band * outs), lambda k: (k, 0, 0)),
        jax.ShapeDtypeStruct((lat_modes, shifts * chans, band * outs), BF),
        [],
        weight.size,
        weight.size * 6,
    )(weight)


def mix_kernel(below_ref, modes_ref, above_ref, weight_ref, table_ref, out_ref, held, mixed):
    lat_modes, deep, wide = weight_ref.shape
    ranks, levels, rows, _ = out_ref.shape
    chans = deep // 3
    band = wide // chans
    step = mixed.shape[1] // lat_modes

    near = [below_ref[0].astype(F32)]
    near += [modes_ref[l].astype(F32) for l in range(levels)]
    near += [above_ref[0].astype(F32)]
    fill = [jnp.zeros((lat_modes, held.shape[0] * 128 - deep), F32)]
    for j in range(band):
        span = slice(j * chans, (j + 1) * chans)
        for l in range(levels):
            row = jnp.concatenate([near[l + d][:, span] for d in range(3)] + fill, axis=1)
            put(held, pl.ds(j * levels + l, lat_modes, stride=step), row)

    for k in range(lat_modes):
        at = slice(k * step, (k + 1) * step)
        lhs = jnp.concatenate([held[p, at, :] for p in range(held.shape[0])], axis=1)
        lhs = lhs[:, :deep].astype(BF)
        put(mixed, at, jnp.dot(lhs, weight_ref[k], preferred_element_type=F32))

    owner = lax.broadcasted_iota(jnp.int32, (lat_modes, wide), 1) // chans
    for l in range(levels):
        value = every(mixed, l, lat_modes, step)
        for j in range(1, band):
            value = jnp.where(owner == j, every(mixed, j * levels + l, lat_modes, step), value)
        value = value.astype(BF)
        back = jnp.dot(
            table_ref[...], jnp.concatenate([value, value], axis=0), preferred_element_type=F32
        )
        out_ref[:, l] = back.astype(BF).reshape(ranks, rows, wide)


def mix(below, modes, above, weight, table, ranks):
    levels, lat_modes, wide = modes.shape
    rows = table.shape[0] // ranks
    deep = weight.shape[1]
    step = (levels * wide * 3 // deep + 7) // 8 * 8
    return call(
        mix_kernel,
        (1,),
        [
            whole(below.shape),
            whole(modes.shape),
            whole(above.shape),
            whole(weight.shape),
            whole(table.shape),
        ],
        whole((ranks, levels, rows, wide)),
        jax.ShapeDtypeStruct((ranks, levels, rows, wide), BF),
        [lanes(lat_modes * step, (deep + 127) // 128 * 128), lanes(lat_modes * step, wide)],
        weight.size * 2 * levels,
        weight.size * 2,
    )(below, modes, above, weight, table)


def finish_kernel(
    batch_at, ahead, back_ref, lon_ref, local_ref, bias_ref, into_ref, down_ref, field_ref, *rest
):
    out_ref, held, coarse, act, hidden, taken, given, take_sem, give_sem = rest[-9:]
    ranks, levels, rows, wide = back_ref.shape
    chans, cells = field_ref.shape[3:]
    band = wide // chans
    hid = down_ref.shape[1]
    total = levels * rows
    steps = total // ahead
    slots, kept = taken.shape[0], given.shape[0]
    tile = min(256, cells)
    spans = [slice(x, x + tile) for x in range(0, cells, tile)]

    def take(t):
        slot = lax.rem(t, slots)
        source = field_ref.at[batch_at, t // rows, lax.rem(t, rows)]
        return pltpu.make_async_copy(source, taken.at[slot], take_sem.at[slot])

    def give(t):
        slot = lax.rem(t, kept)
        target = out_ref.at[batch_at, t // rows, lax.rem(t, rows)]
        return pltpu.make_async_copy(given.at[slot], target, give_sem.at[slot])

    for t in range(min(slots - ahead, total)):
        take(jnp.int32(t)).start()

    for l in range(levels):
        put(
            held,
            slice(l * ranks * rows, (l + 1) * ranks * rows),
            back_ref[:, l].astype(F32).reshape(ranks * rows, wide),
        )

    def prepare(u, t):
        t = jnp.minimum(t, total - 1)
        piece = every(held, (t // rows) * (ranks * rows) + lax.rem(t, rows), ranks, rows)
        stacked = jnp.concatenate(
            [piece[:, j * chans : (j + 1) * chans] for j in range(band)], axis=0
        )
        coarse[u] = jnp.concatenate([stacked.T.astype(BF), local_ref[...]], axis=1)

    def first(u, slot, span):
        both = jnp.concatenate([lon_ref[:, span], taken[slot, :, span]], axis=0)
        return jnp.dot(coarse[u], both, preferred_element_type=F32)

    def store_act(u, span, value):
        value = value + bias_ref[...]
        half = 0.5 * value
        act[u, :, span] = (half + half * lax.erf(value * math.sqrt(0.5))).astype(BF)

    def last(u, slot, into, span):
        down = jnp.dot(down_ref[...], hidden[u, :, span], preferred_element_type=F32)
        given[into, :, span] = (taken[slot, :, span].astype(F32) + down).astype(BF)

    for u in range(ahead):
        prepare(u, jnp.int32(u))
    for u in range(ahead):
        take(jnp.int32(u)).wait()
        for span in spans:
            store_act(u, span, first(u, u, span))
    for u in range(ahead):
        prepare(u, jnp.int32(ahead + u))

    def one(step, carry):
        t = step * ahead

        @pl.when(step + 1 < steps)
        def _():
            for u in range(ahead):
                take(t + ahead + u).wait()

        @pl.when(t - ahead - kept >= 0)
        def _():
            for u in range(ahead):
                give(t - ahead - kept + u).wait()

        for u in range(ahead):
            before = t - ahead + u + slots * kept
            for span in spans:
                both = jnp.dot(into_ref[...], act[u, :, span], preferred_element_type=F32)
                last(u, lax.rem(before, slots), lax.rem(before, kept), span)
                value = first(u, lax.rem(t + ahead + u, slots), span)
                half = both[:hid]
                hidden[u, :, span] = ((half + half * jnp.tanh(half)) * both[hid:]).astype(BF)
                store_act(u, span, value)
            prepare(u, t + 2 * ahead + u)

        @pl.when(step > 0)
        def _():
            for u in range(ahead):
                give(t - ahead + u).start()

        @pl.when(t - ahead + slots < total)
        def _():
            for u in range(ahead):
                take(t - ahead + slots + u).start()

        return carry

    lax.fori_loop(0, steps, one, 0)
    for u in range(ahead):
        t = total - ahead + u
        if t >= kept:
            give(jnp.int32(t - kept)).wait()
        for span in spans:
            last(u, t % slots, t % kept, span)
        give(jnp.int32(t)).start()
    for t in range(max(total - kept, 0), total):
        give(jnp.int32(t)).wait()


def finish(field, back, lon_rows, local, bias, into, down, batch_at, earlier, ahead=2):
    batch, levels, rows, chans, cells = field.shape
    ranks, _, _, wide = back.shape
    modes = lon_rows.shape[0]
    slots, kept = 8 * ahead, 2 * ahead
    operands = [back, lon_rows, local, bias, into, down, field]
    anywhere = pl.BlockSpec(memory_space=pl.ANY)
    in_specs = [whole(x.shape) for x in operands[:-1]] + [anywhere]
    kw = {}
    if earlier is not None:
        operands.append(earlier)
        in_specs.append(anywhere)
        kw["input_output_aliases"] = {7: 0}
    return call(
        functools.partial(finish_kernel, batch_at, ahead),
        (1,),
        in_specs,
        anywhere,
        jax.ShapeDtypeStruct(field.shape, BF),
        [
            lanes(levels * ranks * rows, wide),
            pltpu.VMEM((ahead, chans, modes + chans), BF),
            pltpu.VMEM((ahead, chans, cells), BF),
            pltpu.VMEM((ahead, down.shape[1], cells), BF),
            pltpu.VMEM((slots, chans, cells), BF),
            pltpu.VMEM((kept, chans, cells), BF),
            pltpu.SemaphoreType.DMA((slots,)),
            pltpu.SemaphoreType.DMA((kept,)),
        ],
        2 * levels * rows * cells * chans * (modes + chans + 3 * down.shape[1]),
        levels * rows * chans * cells * 4,
        **kw,
    )(*operands)


def neighbours(modes, sides):
    if sides == 2:
        lower = lax.axis_index("lev") == 0
        got = lax.ppermute(
            jnp.where(lower, modes[-1:], modes[:1]), "lev", [(0, 1), (1, 0)]
        )
        none = jnp.zeros_like(got)
        return jnp.where(lower, none, got), jnp.where(lower, got, none)
    below = lax.ppermute(modes[-1:], "lev", [(i, i + 1) for i in range(sides - 1)])
    above = lax.ppermute(modes[:1], "lev", [(i + 1, i) for i in range(sides - 1)])
    return below, above


def body(field, spectral_weight, local_weight, local_bias, gate_weight, up_weight, down_weight):
    batch, levels, rows, chans, cells = field.shape
    ranks = lax.axis_size("rows")
    sides = lax.axis_size("lev")
    lat_modes = spectral_weight.shape[1]
    band = spectral_weight.shape[2]
    lon_modes = band * ranks
    lon_rows = cas_table(cells, lon_modes).astype(ml_dtypes.bfloat16).T
    lon_rows = lon_rows.reshape(ranks, band, cells).swapaxes(0, 1).reshape(lon_modes, cells)
    lon_rows = jnp.asarray(np.ascontiguousarray(lon_rows))
    high, low = split(cas_table(rows * ranks, lat_modes))
    gather_table = jnp.asarray(np.concatenate([high.T, low.T], axis=0))
    spread_table = jnp.asarray(np.concatenate([high, low], axis=1))

    into = jnp.concatenate([gate_weight * BF(0.5), up_weight], axis=1).T
    down = down_weight.T
    local = local_weight.T
    bias = jnp.broadcast_to(local_bias[:, None], (chans, min(256, cells)))

    weight = arrange(spectral_weight)
    sent = [forward(field, lon_rows, b, ranks) for b in range(batch)]
    backs = []
    for b in range(batch):
        along = lax.all_to_all(sent[b], "rows", 0, 0, tiled=True)
        if b == 0:
            along, weight = lax.optimization_barrier((along, weight))
        modes = to_modes(gather_table, along)
        if b + 1 < batch:
            modes, sent[b + 1] = lax.optimization_barrier((modes, sent[b + 1]))
        below, above = neighbours(modes, sides)
        back = mix(below, modes, above, weight, spread_table, ranks)
        backs.append(lax.all_to_all(back, "rows", 0, 0, tiled=True))
    result = None
    for b in range(batch):
        result = finish(field, backs[b], lon_rows, local, bias, into, down, b, result)
    return result


def solution(mesh):
    return jax.shard_map(
        body,
        mesh=mesh,
        in_specs=(
            P(None, "lev", "rows", None, None),
            P(None, None, "rows", None, None),
            P(),
            P(),
            P(),
            P(),
            P(),
        ),
        out_specs=P(None, "lev", "rows", None, None),
        check_vma=False,
    )
```

```python
import functools
import math

import jax
import jax.numpy as jnp
import ml_dtypes
import numpy as np
from jax import lax
from jax.experimental import pallas as pl
from jax.experimental.pallas import tpu as pltpu
from jax.sharding import PartitionSpec as P

BF = jnp.bfloat16
F32 = jnp.float32
F8 = jnp.float8_e4m3fn
NT = (((1,), (1,)), ((), ()))


def cas_table(count, modes):
    turns = np.arange(count)[:, None] * (np.arange(modes)[None, :] - modes // 2) % count
    angle = 2.0 * math.pi / count * turns
    return ((np.cos(angle) + np.sin(angle)) / math.sqrt(count)).astype(np.float32)


def split(table):
    high = table.astype(ml_dtypes.bfloat16)
    low = (table - high.astype(np.float32)).astype(ml_dtypes.bfloat16)
    return high, low


def call(kernel, grid, in_specs, out_specs, out_shape, scratch, flops, moved, room=48, **kw):
    return pl.pallas_call(
        kernel,
        grid=grid,
        in_specs=in_specs,
        out_specs=out_specs,
        out_shape=out_shape,
        scratch_shapes=scratch,
        compiler_params=pltpu.CompilerParams(
            dimension_semantics=("arbitrary",) * len(grid), vmem_limit_bytes=room * 2**20
        ),
        cost_estimate=pl.CostEstimate(flops=flops, bytes_accessed=moved, transcendentals=0),
        **kw,
    )


def power(bound):
    scale, back = jnp.full_like(bound, 2.0**-40), jnp.full_like(bound, 2.0**40)
    for step in (64, 32, 16, 8, 4, 2, 1):
        more = scale * 2.0**step
        fits = bound * more <= 256.0
        scale = jnp.where(fits, more, scale)
        back = jnp.where(fits, back * 2.0**-step, back)
    return scale, back


def pieces(value):
    high = value.astype(F8)
    return high, (value - high.astype(value.dtype)).astype(F8)


def lanes(rows, wide):
    return pltpu.VMEM((wide // 128, rows, 128), F32)


def every(ref, start, size, stride):
    return jnp.concatenate(
        [ref[p, pl.ds(start, size, stride=stride), :] for p in range(ref.shape[0])], axis=1
    )


def put(ref, at, value):
    for p in range(ref.shape[0]):
        ref[p, at, :] = value[:, p * 128 : (p + 1) * 128]


def whole(shape):
    return pl.BlockSpec(shape, lambda *_: (0,) * len(shape))


def forward_kernel(ranks, field_ref, lon_ref, out_ref, loud_ref, held):
    _, _, rows, chans, cells = field_ref.shape
    modes = lon_ref.shape[0]
    band = modes // ranks
    values = lax.dot_general(
        lon_ref[...], field_ref[0, 0].reshape(rows * chans, cells), NT, preferred_element_type=F32
    )
    for n in range(rows):
        piece = values[:, n * chans : (n + 1) * chans]
        row = jnp.concatenate([piece[j * ranks : (j + 1) * ranks] for j in range(band)], axis=1)
        put(held, pl.ds(n * ranks, ranks), row)
    for r in range(ranks):
        out_ref[r, 0] = every(held, r, rows, ranks).astype(BF)
    size = jnp.abs(field_ref[0, 0]).reshape(rows, chans // 16, 16, cells)
    size = functools.reduce(jnp.maximum, [size[:, i] for i in range(chans // 16)])
    size = functools.reduce(jnp.maximum, [size[..., x : x + 128] for x in range(0, cells, 128)])
    size = jnp.max(size.astype(F32), axis=(1, 2), keepdims=True)
    loud_ref[0] = jnp.broadcast_to(size, (rows, 1, 128)).reshape(rows, 128)


def forward(field, lon_rows, batch_at, ranks):
    _, levels, rows, chans, cells = field.shape
    modes = lon_rows.shape[0]
    wide = modes // ranks * chans
    return call(
        functools.partial(forward_kernel, ranks),
        (levels,),
        [
            pl.BlockSpec((1, 1, rows, chans, cells), lambda l: (batch_at, l, 0, 0, 0)),
            whole((modes, cells)),
        ],
        [
            pl.BlockSpec((ranks, 1, rows, wide), lambda l: (0, l, 0, 0)),
            pl.BlockSpec((1, rows, 128), lambda l: (l, 0, 0)),
        ],
        [
            jax.ShapeDtypeStruct((ranks, levels, rows, wide), BF),
            jax.ShapeDtypeStruct((levels, rows, 128), F32),
        ],
        [lanes(rows * ranks, wide)],
        2 * levels * rows * chans * cells * modes,
        levels * rows * chans * cells * 2,
        room=60,
    )(field, lon_rows)


def modes_kernel(table_ref, along_ref, out_ref):
    ranks, levels, rows, wide = along_ref.shape
    count = out_ref.shape[1]
    for l in range(levels):
        both = jnp.dot(
            table_ref[...],
            along_ref[:, l].reshape(ranks * rows, wide),
            preferred_element_type=F32,
        )
        out_ref[l] = (both[:count] + both[count:]).astype(BF)


def to_modes(table, along):
    ranks, levels, rows, wide = along.shape
    count = table.shape[0] // 2
    return call(
        modes_kernel,
        (1,),
        [whole(table.shape), whole(along.shape)],
        whole((levels, count, wide)),
        jax.ShapeDtypeStruct((levels, count, wide), BF),
        [],
        2 * levels * 2 * count * ranks * rows * wide,
        along.size * 2,
    )(table, along)


def arrange_kernel(weight_ref, out_ref):
    shifts, part, band, chans, _ = weight_ref.shape
    for k in range(part):
        for d in range(shifts):
            out_ref[k, d * chans : (d + 1) * chans, :] = jnp.concatenate(
                [weight_ref[d, k, j] for j in range(band)], axis=1
            )


def arrange(weight, part=32):
    shifts, lat_modes, band, chans, outs = weight.shape
    part = math.gcd(part, lat_modes)
    return call(
        arrange_kernel,
        (lat_modes // part,),
        [pl.BlockSpec((shifts, part, band, chans, outs), lambda k: (0, k, 0, 0, 0))],
        pl.BlockSpec((part, shifts * chans, band * outs), lambda k: (k, 0, 0)),
        jax.ShapeDtypeStruct((lat_modes, shifts * chans, band * outs), BF),
        [],
        weight.size,
        weight.size * 6,
    )(weight)


def mix_kernel(below_ref, modes_ref, above_ref, weight_ref, table_ref, out_ref, held, mixed):
    lat_modes, deep, wide = weight_ref.shape
    ranks, levels, rows, _ = out_ref.shape
    chans = deep // 3
    band = wide // chans
    step = mixed.shape[1] // lat_modes

    near = [below_ref[0].astype(F32)]
    near += [modes_ref[l].astype(F32) for l in range(levels)]
    near += [above_ref[0].astype(F32)]
    fill = [jnp.zeros((lat_modes, held.shape[0] * 128 - deep), F32)]
    for j in range(band):
        span = slice(j * chans, (j + 1) * chans)
        for l in range(levels):
            row = jnp.concatenate([near[l + d][:, span] for d in range(3)] + fill, axis=1)
            put(held, pl.ds(j * levels + l, lat_modes, stride=step), row)

    for k in range(lat_modes):
        at = slice(k * step, (k + 1) * step)
        lhs = jnp.concatenate([held[p, at, :] for p in range(held.shape[0])], axis=1)
        lhs = lhs[:, :deep].astype(BF)
        put(mixed, at, jnp.dot(lhs, weight_ref[k], preferred_element_type=F32))

    owner = lax.broadcasted_iota(jnp.int32, (lat_modes, wide), 1) // chans
    for l in range(levels):
        value = every(mixed, l, lat_modes, step)
        for j in range(1, band):
            value = jnp.where(owner == j, every(mixed, j * levels + l, lat_modes, step), value)
        value = value.astype(BF)
        back = jnp.dot(
            table_ref[...], jnp.concatenate([value, value], axis=0), preferred_element_type=F32
        )
        out_ref[:, l] = back.astype(BF).reshape(ranks, rows, wide)


def mix(below, modes, above, weight, table, ranks):
    levels, lat_modes, wide = modes.shape
    rows = table.shape[0] // ranks
    deep = weight.shape[1]
    step = (levels * wide * 3 // deep + 7) // 8 * 8
    return call(
        mix_kernel,
        (1,),
        [
            whole(below.shape),
            whole(modes.shape),
            whole(above.shape),
            whole(weight.shape),
            whole(table.shape),
        ],
        whole((ranks, levels, rows, wide)),
        jax.ShapeDtypeStruct((ranks, levels, rows, wide), BF),
        [lanes(lat_modes * step, (deep + 127) // 128 * 128), lanes(lat_modes * step, wide)],
        weight.size * 2 * levels,
        weight.size * 2,
    )(below, modes, above, weight, table)


def finish_kernel(
    batch_at, ahead, reach, back_ref, lon_ref, local_ref, bias_ref, into_ref, down_ref, loud_ref,
    field_ref, *rest
):
    (
        out_ref, held, coarse, act, hidden, into, act_scale, gate_scale, up_scale,
        taken, given, take_sem, give_sem,
    ) = rest[-13:]
    ranks, levels, rows, wide = back_ref.shape
    chans, cells = field_ref.shape[3:]
    band = wide // chans
    hid = down_ref.shape[1]
    total = levels * rows
    steps = total // ahead
    slots, kept = taken.shape[0], given.shape[0]
    tile = min(256, cells)
    spans = [slice(x, x + tile) for x in range(0, cells, tile)]

    def take(t):
        slot = lax.rem(t, slots)
        source = field_ref.at[batch_at, t // rows, lax.rem(t, rows)]
        return pltpu.make_async_copy(source, taken.at[slot], take_sem.at[slot])

    def give(t):
        slot = lax.rem(t, kept)
        target = out_ref.at[batch_at, t // rows, lax.rem(t, rows)]
        return pltpu.make_async_copy(given.at[slot], target, give_sem.at[slot])

    for t in range(min(slots - ahead, total)):
        take(jnp.int32(t)).start()

    for l in range(levels):
        put(
            held,
            slice(l * ranks * rows, (l + 1) * ranks * rows),
            back_ref[:, l].astype(F32).reshape(ranks * rows, wide),
        )

    def largest(x):
        return jnp.max(jnp.abs(x.astype(F32)), axis=(0, 1), keepdims=True)

    inverse = []
    for part in range(2):
        weight = into_ref[part * hid : (part + 1) * hid].astype(F32)
        scale, undo = power(largest(weight))
        inverse.append(undo)
        high, low = pieces(weight * scale)
        high, low = high.astype(F32), low.astype(F32)
        into[part * hid : (part + 1) * hid] = jnp.concatenate(
            [high, high, low, low], axis=1
        ).astype(F8)
    mixing = jnp.max(
        jnp.sum(jnp.abs(local_ref[...].astype(F32)), axis=1, keepdims=True), axis=0, keepdims=True
    )
    offset = largest(bias_ref[...])
    for l in range(levels):
        coarsest = functools.reduce(jnp.maximum, [jnp.abs(back_ref[r, l]) for r in range(ranks)])
        coarsest = jnp.max(coarsest.astype(F32), axis=1, keepdims=True)
        bound = 1.01 * (coarsest * reach + loud_ref[l] * mixing + offset)
        scale, undo = power(jnp.concatenate([bound] * (tile // 128), axis=1))
        at = slice(l * rows, (l + 1) * rows)
        act_scale[at] = 0.5 * scale
        gate_scale[at] = undo * inverse[0]
        up_scale[at] = undo * inverse[1]

    def prepare(u, t):
        t = jnp.minimum(t, total - 1)
        piece = every(held, (t // rows) * (ranks * rows) + lax.rem(t, rows), ranks, rows)
        stacked = jnp.concatenate(
            [piece[:, j * chans : (j + 1) * chans] for j in range(band)], axis=0
        )
        coarse[u] = jnp.concatenate([stacked.T.astype(BF), local_ref[...]], axis=1)

    def first(u, slot, span):
        both = jnp.concatenate([lon_ref[:, span], taken[slot, :, span]], axis=0)
        return jnp.dot(coarse[u], both, preferred_element_type=F32)

    def store_act(u, t, span, value):
        value = value + bias_ref[...]
        half = value * act_scale[pl.ds(t, 1), :]
        high, low = pieces((half + half * lax.erf(value * math.sqrt(0.5))).astype(BF))
        act[u, :chans, span] = high
        act[u, chans:, span] = low

    def last(u, t, slot, kept_at, span):
        down = jnp.dot(down_ref[...], hidden[u, :, span], preferred_element_type=F32)
        down = down * up_scale[pl.ds(t, 1), :]
        given[kept_at, :, span] = (taken[slot, :, span].astype(F32) + down).astype(BF)

    for u in range(ahead):
        prepare(u, jnp.int32(u))
    for u in range(ahead):
        take(jnp.int32(u)).wait()
        for span in spans:
            store_act(u, u, span, first(u, u, span))
    for u in range(ahead):
        prepare(u, jnp.int32(ahead + u))

    def one(step, carry):
        t = step * ahead

        @pl.when(step + 1 < steps)
        def _():
            for u in range(ahead):
                take(t + ahead + u).wait()

        @pl.when(t - ahead - kept >= 0)
        def _():
            for u in range(ahead):
                give(t - ahead - kept + u).wait()

        for u in range(ahead):
            before = t - ahead + u + slots * kept
            earlier = jnp.maximum(t - ahead + u, 0)
            later = jnp.minimum(t + ahead + u, total - 1)
            gate_undo = gate_scale[pl.ds(t + u, 1), :].astype(BF)
            for span in spans:
                ours = act[u, :, span]
                ours = jnp.concatenate([ours, ours], axis=0)
                both = jnp.dot(into[...], ours, preferred_element_type=F32)
                last(u, earlier, lax.rem(before, slots), lax.rem(before, kept), span)
                value = first(u, lax.rem(t + ahead + u, slots), span)
                half = both[:hid].astype(BF) * gate_undo
                hidden[u, :, span] = half * (1 + jnp.tanh(half)) * both[hid:].astype(BF)
                store_act(u, later, span, value)
            prepare(u, t + 2 * ahead + u)

        @pl.when(step > 0)
        def _():
            for u in range(ahead):
                give(t - ahead + u).start()

        @pl.when(t - ahead + slots < total)
        def _():
            for u in range(ahead):
                take(t - ahead + slots + u).start()

        return carry

    lax.fori_loop(0, steps, one, 0)
    for u in range(ahead):
        t = total - ahead + u
        if t >= kept:
            give(jnp.int32(t - kept)).wait()
        for span in spans:
            last(u, t, t % slots, t % kept, span)
        give(jnp.int32(t)).start()
    for t in range(max(total - kept, 0), total):
        give(jnp.int32(t)).wait()


def finish(field, back, lon_rows, local, bias, into, down, loud, reach, batch_at, earlier, ahead=2):
    batch, levels, rows, chans, cells = field.shape
    ranks, _, _, wide = back.shape
    modes = lon_rows.shape[0]
    slots, kept = 8 * ahead, 2 * ahead
    operands = [back, lon_rows, local, bias, into, down, loud, field]
    anywhere = pl.BlockSpec(memory_space=pl.ANY)
    in_specs = [whole(x.shape) for x in operands[:-1]] + [anywhere]
    kw = {}
    if earlier is not None:
        operands.append(earlier)
        in_specs.append(anywhere)
        kw["input_output_aliases"] = {8: 0}
    return call(
        functools.partial(finish_kernel, batch_at, ahead, reach),
        (1,),
        in_specs,
        anywhere,
        jax.ShapeDtypeStruct(field.shape, BF),
        [
            lanes(levels * ranks * rows, wide),
            pltpu.VMEM((ahead, chans, modes + chans), BF),
            pltpu.VMEM((ahead, 2 * chans, cells), F8),
            pltpu.VMEM((ahead, down.shape[1], cells), BF),
            pltpu.VMEM((2 * down.shape[1], 4 * chans), F8),
            *[pltpu.VMEM((levels * rows, min(256, cells)), F32)] * 3,
            pltpu.VMEM((slots, chans, cells), BF),
            pltpu.VMEM((kept, chans, cells), BF),
            pltpu.SemaphoreType.DMA((slots,)),
            pltpu.SemaphoreType.DMA((kept,)),
        ],
        2 * levels * rows * cells * chans * (modes + chans + 3 * down.shape[1]),
        levels * rows * chans * cells * 4,
        **kw,
    )(*operands)


def neighbours(modes, sides):
    if sides == 2:
        lower = lax.axis_index("lev") == 0
        got = lax.ppermute(
            jnp.where(lower, modes[-1:], modes[:1]), "lev", [(0, 1), (1, 0)]
        )
        none = jnp.zeros_like(got)
        return jnp.where(lower, none, got), jnp.where(lower, got, none)
    below = lax.ppermute(modes[-1:], "lev", [(i, i + 1) for i in range(sides - 1)])
    above = lax.ppermute(modes[:1], "lev", [(i + 1, i) for i in range(sides - 1)])
    return below, above


def body(field, spectral_weight, local_weight, local_bias, gate_weight, up_weight, down_weight):
    batch, levels, rows, chans, cells = field.shape
    ranks = lax.axis_size("rows")
    sides = lax.axis_size("lev")
    lat_modes = spectral_weight.shape[1]
    band = spectral_weight.shape[2]
    lon_modes = band * ranks
    lon_rows = cas_table(cells, lon_modes).astype(ml_dtypes.bfloat16).T
    lon_rows = lon_rows.reshape(ranks, band, cells).swapaxes(0, 1).reshape(lon_modes, cells)
    reach = float(np.abs(lon_rows.astype(np.float32)).sum(axis=0).max())
    lon_rows = jnp.asarray(np.ascontiguousarray(lon_rows))
    high, low = split(cas_table(rows * ranks, lat_modes))
    gather_table = jnp.asarray(np.concatenate([high.T, low.T], axis=0))
    spread_table = jnp.asarray(np.concatenate([high, low], axis=1))

    into = jnp.concatenate([gate_weight * BF(0.5), up_weight], axis=1).T
    down = down_weight.T
    local = local_weight.T
    bias = jnp.broadcast_to(local_bias[:, None], (chans, min(256, cells)))

    weight = arrange(spectral_weight)
    sent, loud = map(list, zip(*[forward(field, lon_rows, b, ranks) for b in range(batch)]))
    backs = []
    for b in range(batch):
        along = lax.all_to_all(sent[b], "rows", 0, 0, tiled=True)
        if b == 0:
            along, weight = lax.optimization_barrier((along, weight))
        modes = to_modes(gather_table, along)
        if b + 1 < batch:
            modes, sent[b + 1] = lax.optimization_barrier((modes, sent[b + 1]))
        below, above = neighbours(modes, sides)
        back = mix(below, modes, above, weight, spread_table, ranks)
        backs.append(lax.all_to_all(back, "rows", 0, 0, tiled=True))
    result = None
    for b in range(batch):
        result = finish(
            field, backs[b], lon_rows, local, bias, into, down, loud[b], reach, b, result
        )
    return result


def solution(mesh):
    return jax.shard_map(
        body,
        mesh=mesh,
        in_specs=(
            P(None, "lev", "rows", None, None),
            P(None, None, "rows", None, None),
            P(),
            P(),
            P(),
            P(),
            P(),
        ),
        out_specs=P(None, "lev", "rows", None, None),
        check_vma=False,
    )
```

```python
import functools
import math

import jax
import jax.numpy as jnp
import ml_dtypes
import numpy as np
from jax import lax
from jax.experimental import pallas as pl
from jax.experimental.pallas import tpu as pltpu
from jax.sharding import PartitionSpec as P

BF = jnp.bfloat16
F32 = jnp.float32
F8 = jnp.float8_e4m3fn
NT = (((1,), (1,)), ((), ()))


def cas_table(count, modes):
    turns = np.arange(count)[:, None] * (np.arange(modes)[None, :] - modes // 2) % count
    angle = 2.0 * math.pi / count * turns
    return ((np.cos(angle) + np.sin(angle)) / math.sqrt(count)).astype(np.float32)


def split(table):
    high = table.astype(ml_dtypes.bfloat16)
    low = (table - high.astype(np.float32)).astype(ml_dtypes.bfloat16)
    return high, low


def call(kernel, grid, in_specs, out_specs, out_shape, scratch, flops, moved, room=48, **kw):
    return pl.pallas_call(
        kernel,
        grid=grid,
        in_specs=in_specs,
        out_specs=out_specs,
        out_shape=out_shape,
        scratch_shapes=scratch,
        compiler_params=pltpu.CompilerParams(
            dimension_semantics=("arbitrary",) * len(grid), vmem_limit_bytes=room * 2**20
        ),
        cost_estimate=pl.CostEstimate(flops=flops, bytes_accessed=moved, transcendentals=0),
        **kw,
    )


def power(bound):
    scale, back = jnp.full_like(bound, 2.0**-40), jnp.full_like(bound, 2.0**40)
    for step in (64, 32, 16, 8, 4, 2, 1):
        more = scale * 2.0**step
        fits = bound * more <= 256.0
        scale = jnp.where(fits, more, scale)
        back = jnp.where(fits, back * 2.0**-step, back)
    return scale, back


def pieces(value):
    high = value.astype(F8)
    return high, (value - high.astype(value.dtype)).astype(F8)


def lanes(size, stride, wide):
    return pltpu.VMEM((wide // 128, (size + 1) * stride, 128), F32)


def every(ref, start, size, stride):
    return jnp.concatenate(
        [ref[p, pl.ds(start, size, stride=stride), :] for p in range(ref.shape[0])], axis=1
    )


def put(ref, at, value):
    for p in range(ref.shape[0]):
        ref[p, at, :] = value[:, p * 128 : (p + 1) * 128]


def whole(shape):
    return pl.BlockSpec(shape, lambda *_: (0,) * len(shape))


def forward_kernel(ranks, field_ref, lon_ref, out_ref, loud_ref, held):
    _, _, rows, chans, cells = field_ref.shape
    modes = lon_ref.shape[0]
    band = modes // ranks
    values = lax.dot_general(
        lon_ref[...], field_ref[0, 0].reshape(rows * chans, cells), NT, preferred_element_type=F32
    )
    for n in range(rows):
        piece = values[:, n * chans : (n + 1) * chans]
        row = jnp.concatenate([piece[j * ranks : (j + 1) * ranks] for j in range(band)], axis=1)
        put(held, pl.ds(n * ranks, ranks), row)
    for r in range(ranks):
        out_ref[r, 0] = every(held, r, rows, ranks).astype(BF)
    size = jnp.abs(field_ref[0, 0]).reshape(rows, chans // 16, 16, cells)
    size = functools.reduce(jnp.maximum, [size[:, i] for i in range(chans // 16)])
    size = functools.reduce(jnp.maximum, [size[..., x : x + 128] for x in range(0, cells, 128)])
    size = jnp.max(size.astype(F32), axis=(1, 2), keepdims=True)
    loud_ref[0] = jnp.broadcast_to(size, (rows, 1, 128)).reshape(rows, 128)


def forward(field, lon_rows, batch_at, ranks):
    _, levels, rows, chans, cells = field.shape
    modes = lon_rows.shape[0]
    wide = modes // ranks * chans
    return call(
        functools.partial(forward_kernel, ranks),
        (levels,),
        [
            pl.BlockSpec((1, 1, rows, chans, cells), lambda l: (batch_at, l, 0, 0, 0)),
            whole((modes, cells)),
        ],
        [
            pl.BlockSpec((ranks, 1, rows, wide), lambda l: (0, l, 0, 0)),
            pl.BlockSpec((1, rows, 128), lambda l: (l, 0, 0)),
        ],
        [
            jax.ShapeDtypeStruct((ranks, levels, rows, wide), BF),
            jax.ShapeDtypeStruct((levels, rows, 128), F32),
        ],
        [lanes(rows, ranks, wide)],
        2 * levels * rows * chans * cells * modes,
        levels * rows * chans * cells * 2,
        room=60,
    )(field, lon_rows)


def modes_kernel(table_ref, along_ref, out_ref):
    ranks, levels, rows, wide = along_ref.shape
    count = out_ref.shape[1]
    for l in range(levels):
        both = jnp.dot(
            table_ref[...],
            along_ref[:, l].reshape(ranks * rows, wide),
            preferred_element_type=F32,
        )
        out_ref[l] = (both[:count] + both[count:]).astype(BF)


def to_modes(table, along):
    ranks, levels, rows, wide = along.shape
    count = table.shape[0] // 2
    return call(
        modes_kernel,
        (1,),
        [whole(table.shape), whole(along.shape)],
        whole((levels, count, wide)),
        jax.ShapeDtypeStruct((levels, count, wide), BF),
        [],
        2 * levels * 2 * count * ranks * rows * wide,
        along.size * 2,
    )(table, along)


def arrange_kernel(weight_ref, out_ref):
    shifts, part, band, chans, _ = weight_ref.shape
    for k in range(part):
        for d in range(shifts):
            out_ref[k, d * chans : (d + 1) * chans, :] = jnp.concatenate(
                [weight_ref[d, k, j] for j in range(band)], axis=1
            )


def arrange(weight, part=32):
    shifts, lat_modes, band, chans, outs = weight.shape
    part = math.gcd(part, lat_modes)
    return call(
        arrange_kernel,
        (lat_modes // part,),
        [pl.BlockSpec((shifts, part, band, chans, outs), lambda k: (0, k, 0, 0, 0))],
        pl.BlockSpec((part, shifts * chans, band * outs), lambda k: (k, 0, 0)),
        jax.ShapeDtypeStruct((lat_modes, shifts * chans, band * outs), BF),
        [],
        weight.size,
        weight.size * 6,
    )(weight)


def mix_kernel(below_ref, modes_ref, above_ref, weight_ref, table_ref, out_ref, held, mixed):
    lat_modes, deep, wide = weight_ref.shape
    ranks, levels, rows, _ = out_ref.shape
    chans = deep // 3
    band = wide // chans
    step = mixed.shape[1] // (lat_modes + 1)

    near = [below_ref[0].astype(F32)]
    near += [modes_ref[l].astype(F32) for l in range(levels)]
    near += [above_ref[0].astype(F32)]
    fill = [jnp.zeros((lat_modes, held.shape[0] * 128 - deep), F32)]
    for j in range(band):
        span = slice(j * chans, (j + 1) * chans)
        for l in range(levels):
            row = jnp.concatenate([near[l + d][:, span] for d in range(3)] + fill, axis=1)
            put(held, pl.ds(j * levels + l, lat_modes, stride=step), row)

    for k in range(lat_modes):
        at = slice(k * step, (k + 1) * step)
        lhs = jnp.concatenate([held[p, at, :] for p in range(held.shape[0])], axis=1)
        lhs = lhs[:, :deep].astype(BF)
        put(mixed, at, jnp.dot(lhs, weight_ref[k], preferred_element_type=F32))

    owner = lax.broadcasted_iota(jnp.int32, (lat_modes, wide), 1) // chans
    for l in range(levels):
        value = every(mixed, l, lat_modes, step)
        for j in range(1, band):
            value = jnp.where(owner == j, every(mixed, j * levels + l, lat_modes, step), value)
        value = value.astype(BF)
        back = jnp.dot(
            table_ref[...], jnp.concatenate([value, value], axis=0), preferred_element_type=F32
        )
        out_ref[:, l] = back.astype(BF).reshape(ranks, rows, wide)


def mix(below, modes, above, weight, table, ranks):
    levels, lat_modes, wide = modes.shape
    rows = table.shape[0] // ranks
    deep = weight.shape[1]
    step = (levels * wide * 3 // deep + 7) // 8 * 8
    return call(
        mix_kernel,
        (1,),
        [
            whole(below.shape),
            whole(modes.shape),
            whole(above.shape),
            whole(weight.shape),
            whole(table.shape),
        ],
        whole((ranks, levels, rows, wide)),
        jax.ShapeDtypeStruct((ranks, levels, rows, wide), BF),
        [lanes(lat_modes, step, (deep + 127) // 128 * 128), lanes(lat_modes, step, wide)],
        weight.size * 2 * levels,
        weight.size * 2,
    )(below, modes, above, weight, table)


def finish_kernel(
    batch_at, ahead, reach, back_ref, lon_ref, local_ref, bias_ref, into_ref, down_ref, loud_ref,
    field_ref, *rest
):
    (
        out_ref, held, coarse, act, hidden, into, act_scale, gate_scale, up_scale,
        taken, given, take_sem, give_sem,
    ) = rest[-13:]
    ranks, levels, rows, wide = back_ref.shape
    chans, cells = field_ref.shape[3:]
    band = wide // chans
    hid = down_ref.shape[1]
    total = levels * rows
    steps = total // ahead
    slots, kept = taken.shape[0], given.shape[0]
    tile = min(256, cells)
    spans = [slice(x, x + tile) for x in range(0, cells, tile)]

    def take(t):
        slot = lax.rem(t, slots)
        source = field_ref.at[batch_at, t // rows, lax.rem(t, rows)]
        return pltpu.make_async_copy(source, taken.at[slot], take_sem.at[slot])

    def give(t):
        slot = lax.rem(t, kept)
        target = out_ref.at[batch_at, t // rows, lax.rem(t, rows)]
        return pltpu.make_async_copy(given.at[slot], target, give_sem.at[slot])

    for t in range(min(slots - ahead, total)):
        take(jnp.int32(t)).start()

    for l in range(levels):
        put(
            held,
            slice(l * ranks * rows, (l + 1) * ranks * rows),
            back_ref[:, l].astype(F32).reshape(ranks * rows, wide),
        )

    def largest(x):
        return jnp.max(jnp.abs(x.astype(F32)), axis=(0, 1), keepdims=True)

    inverse = []
    for part in range(2):
        weight = into_ref[part * hid : (part + 1) * hid].astype(F32)
        scale, undo = power(largest(weight))
        inverse.append(undo)
        high, low = pieces(weight * scale)
        high, low = high.astype(F32), low.astype(F32)
        into[part * hid : (part + 1) * hid] = jnp.concatenate(
            [high, high, low, low], axis=1
        ).astype(F8)
    mixing = jnp.max(
        jnp.sum(jnp.abs(local_ref[...].astype(F32)), axis=1, keepdims=True), axis=0, keepdims=True
    )
    offset = largest(bias_ref[...])
    for l in range(levels):
        coarsest = functools.reduce(jnp.maximum, [jnp.abs(back_ref[r, l]) for r in range(ranks)])
        coarsest = jnp.max(coarsest.astype(F32), axis=1, keepdims=True)
        bound = 1.01 * (coarsest * reach + loud_ref[l] * mixing + offset)
        scale, undo = power(jnp.concatenate([bound] * (tile // 128), axis=1))
        at = slice(l * rows, (l + 1) * rows)
        act_scale[at] = 0.5 * scale
        gate_scale[at] = undo * inverse[0]
        up_scale[at] = undo * inverse[1]

    def prepare(u, t):
        t = jnp.minimum(t, total - 1)
        piece = every(held, (t // rows) * (ranks * rows) + lax.rem(t, rows), ranks, rows)
        stacked = jnp.concatenate(
            [piece[:, j * chans : (j + 1) * chans] for j in range(band)], axis=0
        )
        coarse[u] = jnp.concatenate([stacked.T.astype(BF), local_ref[...]], axis=1)

    def first(u, slot, span):
        both = jnp.concatenate([lon_ref[:, span], taken[slot, :, span]], axis=0)
        return jnp.dot(coarse[u], both, preferred_element_type=F32)

    def store_act(u, t, span, value):
        value = value + bias_ref[...]
        half = value * act_scale[pl.ds(t, 1), :]
        high, low = pieces((half + half * lax.erf(value * math.sqrt(0.5))).astype(BF))
        act[u, :chans, span] = high
        act[u, chans:, span] = low

    def last(u, t, slot, kept_at, span):
        down = jnp.dot(down_ref[...], hidden[u, :, span], preferred_element_type=F32)
        down = down * up_scale[pl.ds(t, 1), :]
        given[kept_at, :, span] = (taken[slot, :, span].astype(F32) + down).astype(BF)

    for u in range(ahead):
        prepare(u, jnp.int32(u))
    for u in range(ahead):
        take(jnp.int32(u)).wait()
        for span in spans:
            store_act(u, u, span, first(u, u, span))
    for u in range(ahead):
        prepare(u, jnp.int32(ahead + u))

    def one(step, carry):
        t = step * ahead

        @pl.when(step + 1 < steps)
        def _():
            for u in range(ahead):
                take(t + ahead + u).wait()

        @pl.when(t - ahead - kept >= 0)
        def _():
            for u in range(ahead):
                give(t - ahead - kept + u).wait()

        for u in range(ahead):
            before = t - ahead + u + slots * kept
            earlier = jnp.maximum(t - ahead + u, 0)
            later = jnp.minimum(t + ahead + u, total - 1)
            gate_undo = gate_scale[pl.ds(t + u, 1), :].astype(BF)
            for span in spans:
                ours = act[u, :, span]
                ours = jnp.concatenate([ours, ours], axis=0)
                both = jnp.dot(into[...], ours, preferred_element_type=F32)
                last(u, earlier, lax.rem(before, slots), lax.rem(before, kept), span)
                value = first(u, lax.rem(t + ahead + u, slots), span)
                half = both[:hid].astype(BF) * gate_undo
                hidden[u, :, span] = half * (1 + jnp.tanh(half)) * both[hid:].astype(BF)
                store_act(u, later, span, value)
            prepare(u, t + 2 * ahead + u)

        @pl.when(step > 0)
        def _():
            for u in range(ahead):
                give(t - ahead + u).start()

        @pl.when(t - ahead + slots < total)
        def _():
            for u in range(ahead):
                take(t - ahead + slots + u).start()

        return carry

    lax.fori_loop(0, steps, one, 0)
    for u in range(ahead):
        t = total - ahead + u
        if t >= kept:
            give(jnp.int32(t - kept)).wait()
        for span in spans:
            last(u, t, t % slots, t % kept, span)
        give(jnp.int32(t)).start()
    for t in range(max(total - kept, 0), total):
        give(jnp.int32(t)).wait()


def finish(field, back, lon_rows, local, bias, into, down, loud, reach, batch_at, earlier, ahead=2):
    batch, levels, rows, chans, cells = field.shape
    ranks, _, _, wide = back.shape
    modes = lon_rows.shape[0]
    slots, kept = 8 * ahead, 2 * ahead
    operands = [back, lon_rows, local, bias, into, down, loud, field]
    anywhere = pl.BlockSpec(memory_space=pl.ANY)
    in_specs = [whole(x.shape) for x in operands[:-1]] + [anywhere]
    kw = {}
    if earlier is not None:
        operands.append(earlier)
        in_specs.append(anywhere)
        kw["input_output_aliases"] = {8: 0}
    return call(
        functools.partial(finish_kernel, batch_at, ahead, reach),
        (1,),
        in_specs,
        anywhere,
        jax.ShapeDtypeStruct(field.shape, BF),
        [
            lanes(levels * ranks, rows, wide),
            pltpu.VMEM((ahead, chans, modes + chans), BF),
            pltpu.VMEM((ahead, 2 * chans, cells), F8),
            pltpu.VMEM((ahead, down.shape[1], cells), BF),
            pltpu.VMEM((2 * down.shape[1], 4 * chans), F8),
            *[pltpu.VMEM((levels * rows, min(256, cells)), F32)] * 3,
            pltpu.VMEM((slots, chans, cells), BF),
            pltpu.VMEM((kept, chans, cells), BF),
            pltpu.SemaphoreType.DMA((slots,)),
            pltpu.SemaphoreType.DMA((kept,)),
        ],
        2 * levels * rows * cells * chans * (modes + chans + 3 * down.shape[1]),
        levels * rows * chans * cells * 4,
        **kw,
    )(*operands)


def neighbours(modes, sides):
    if sides == 2:
        lower = lax.axis_index("lev") == 0
        got = lax.ppermute(
            jnp.where(lower, modes[-1:], modes[:1]), "lev", [(0, 1), (1, 0)]
        )
        none = jnp.zeros_like(got)
        return jnp.where(lower, none, got), jnp.where(lower, got, none)
    below = lax.ppermute(modes[-1:], "lev", [(i, i + 1) for i in range(sides - 1)])
    above = lax.ppermute(modes[:1], "lev", [(i + 1, i) for i in range(sides - 1)])
    return below, above


def body(field, spectral_weight, local_weight, local_bias, gate_weight, up_weight, down_weight):
    batch, levels, rows, chans, cells = field.shape
    ranks = lax.axis_size("rows")
    sides = lax.axis_size("lev")
    lat_modes = spectral_weight.shape[1]
    band = spectral_weight.shape[2]
    lon_modes = band * ranks
    lon_rows = cas_table(cells, lon_modes).astype(ml_dtypes.bfloat16).T
    lon_rows = lon_rows.reshape(ranks, band, cells).swapaxes(0, 1).reshape(lon_modes, cells)
    reach = float(np.abs(lon_rows.astype(np.float32)).sum(axis=0).max())
    lon_rows = jnp.asarray(np.ascontiguousarray(lon_rows))
    high, low = split(cas_table(rows * ranks, lat_modes))
    gather_table = jnp.asarray(np.concatenate([high.T, low.T], axis=0))
    spread_table = jnp.asarray(np.concatenate([high, low], axis=1))

    into = jnp.concatenate([gate_weight * BF(0.5), up_weight], axis=1).T
    down = down_weight.T
    local = local_weight.T
    bias = jnp.broadcast_to(local_bias[:, None], (chans, min(256, cells)))

    weight = arrange(spectral_weight)
    sent, loud = map(list, zip(*[forward(field, lon_rows, b, ranks) for b in range(batch)]))
    backs = []
    for b in range(batch):
        along = lax.all_to_all(sent[b], "rows", 0, 0, tiled=True)
        if b == 0:
            along, weight = lax.optimization_barrier((along, weight))
        modes = to_modes(gather_table, along)
        if b + 1 < batch:
            modes, sent[b + 1] = lax.optimization_barrier((modes, sent[b + 1]))
        below, above = neighbours(modes, sides)
        back = mix(below, modes, above, weight, spread_table, ranks)
        backs.append(lax.all_to_all(back, "rows", 0, 0, tiled=True))
    result = None
    for b in range(batch):
        result = finish(
            field, backs[b], lon_rows, local, bias, into, down, loud[b], reach, b, result
        )
    return result


def solution(mesh):
    return jax.shard_map(
        body,
        mesh=mesh,
        in_specs=(
            P(None, "lev", "rows", None, None),
            P(None, None, "rows", None, None),
            P(),
            P(),
            P(),
            P(),
            P(),
        ),
        out_specs=P(None, "lev", "rows", None, None),
        check_vma=False,
    )
```

```python
import functools
import math

import jax
import jax.numpy as jnp
import ml_dtypes
import numpy as np
from jax import lax
from jax.experimental import pallas as pl
from jax.experimental.pallas import tpu as pltpu
from jax.sharding import PartitionSpec as P

BF = jnp.bfloat16
F32 = jnp.float32
F8 = jnp.float8_e4m3fn
NT = (((1,), (1,)), ((), ()))


def cas_table(count, modes):
    turns = np.arange(count)[:, None] * (np.arange(modes)[None, :] - modes // 2) % count
    angle = 2.0 * math.pi / count * turns
    return ((np.cos(angle) + np.sin(angle)) / math.sqrt(count)).astype(np.float32)


def split(table):
    high = table.astype(ml_dtypes.bfloat16)
    low = (table - high.astype(np.float32)).astype(ml_dtypes.bfloat16)
    return high, low


def call(kernel, grid, in_specs, out_specs, out_shape, scratch, flops, moved, room=48, **kw):
    return pl.pallas_call(
        kernel,
        grid=grid,
        in_specs=in_specs,
        out_specs=out_specs,
        out_shape=out_shape,
        scratch_shapes=scratch,
        compiler_params=pltpu.CompilerParams(
            dimension_semantics=("arbitrary",) * len(grid), vmem_limit_bytes=room * 2**20
        ),
        cost_estimate=pl.CostEstimate(flops=flops, bytes_accessed=moved, transcendentals=0),
        **kw,
    )


def power(bound):
    scale, back = jnp.full_like(bound, 2.0**-40), jnp.full_like(bound, 2.0**40)
    for step in (64, 32, 16, 8, 4, 2, 1):
        more = scale * 2.0**step
        fits = bound * more <= 256.0
        scale = jnp.where(fits, more, scale)
        back = jnp.where(fits, back * 2.0**-step, back)
    return scale, back


def pieces(value):
    high = value.astype(F8)
    return high, (value - high.astype(value.dtype)).astype(F8)


def lanes(size, stride, wide):
    return pltpu.VMEM((wide // 128, (size + 1) * stride, 128), F32)


def every(ref, start, size, stride):
    return jnp.concatenate(
        [ref[p, pl.ds(start, size, stride=stride), :] for p in range(ref.shape[0])], axis=1
    )


def put(ref, at, value):
    for p in range(ref.shape[0]):
        ref[p, at, :] = value[:, p * 128 : (p + 1) * 128]


def whole(shape):
    return pl.BlockSpec(shape, lambda *_: (0,) * len(shape))


def forward_kernel(ranks, field_ref, lon_ref, out_ref, loud_ref, held):
    _, _, rows, chans, cells = field_ref.shape
    modes = lon_ref.shape[0]
    band = modes // ranks
    values = lax.dot_general(
        lon_ref[...], field_ref[0, 0].reshape(rows * chans, cells), NT, preferred_element_type=F32
    )
    for n in range(rows):
        piece = values[:, n * chans : (n + 1) * chans]
        row = jnp.concatenate([piece[j * ranks : (j + 1) * ranks] for j in range(band)], axis=1)
        put(held, pl.ds(n * ranks, ranks), row)
    for r in range(ranks):
        out_ref[r, 0] = every(held, r, rows, ranks).astype(BF)
    size = jnp.abs(field_ref[0, 0]).reshape(rows, chans // 16, 16, cells)
    size = functools.reduce(jnp.maximum, [size[:, i] for i in range(chans // 16)])
    size = functools.reduce(jnp.maximum, [size[..., x : x + 128] for x in range(0, cells, 128)])
    size = jnp.max(size.astype(F32), axis=(1, 2), keepdims=True)
    loud_ref[0] = jnp.broadcast_to(size, (rows, 1, 128)).reshape(rows, 128)


def forward(field, lon_rows, batch_at, ranks):
    _, levels, rows, chans, cells = field.shape
    modes = lon_rows.shape[0]
    wide = modes // ranks * chans
    return call(
        functools.partial(forward_kernel, ranks),
        (levels,),
        [
            pl.BlockSpec((1, 1, rows, chans, cells), lambda l: (batch_at, l, 0, 0, 0)),
            whole((modes, cells)),
        ],
        [
            pl.BlockSpec((ranks, 1, rows, wide), lambda l: (0, l, 0, 0)),
            pl.BlockSpec((1, rows, 128), lambda l: (l, 0, 0)),
        ],
        [
            jax.ShapeDtypeStruct((ranks, levels, rows, wide), BF),
            jax.ShapeDtypeStruct((levels, rows, 128), F32),
        ],
        [lanes(rows, ranks, wide)],
        2 * levels * rows * chans * cells * modes,
        levels * rows * chans * cells * 2,
        room=60,
    )(field, lon_rows)


def modes_kernel(table_ref, along_ref, out_ref):
    ranks, levels, rows, wide = along_ref.shape
    count = out_ref.shape[1]
    for l in range(levels):
        both = jnp.dot(
            table_ref[...],
            along_ref[:, l].reshape(ranks * rows, wide),
            preferred_element_type=F32,
        )
        out_ref[l] = (both[:count] + both[count:]).astype(BF)


def to_modes(table, along):
    ranks, levels, rows, wide = along.shape
    count = table.shape[0] // 2
    return call(
        modes_kernel,
        (1,),
        [whole(table.shape), whole(along.shape)],
        whole((levels, count, wide)),
        jax.ShapeDtypeStruct((levels, count, wide), BF),
        [],
        2 * levels * 2 * count * ranks * rows * wide,
        along.size * 2,
    )(table, along)


def arrange_kernel(weight_ref, out_ref):
    shifts, part, band, chans, _ = weight_ref.shape
    for k in range(part):
        for d in range(shifts):
            out_ref[k, d * chans : (d + 1) * chans, :] = jnp.concatenate(
                [weight_ref[d, k, j] for j in range(band)], axis=1
            )


def arrange(weight, part=32):
    shifts, lat_modes, band, chans, outs = weight.shape
    part = math.gcd(part, lat_modes)
    return call(
        arrange_kernel,
        (lat_modes // part,),
        [pl.BlockSpec((shifts, part, band, chans, outs), lambda k: (0, k, 0, 0, 0))],
        pl.BlockSpec((part, shifts * chans, band * outs), lambda k: (k, 0, 0)),
        jax.ShapeDtypeStruct((lat_modes, shifts * chans, band * outs), BF),
        [],
        weight.size,
        weight.size * 6,
    )(weight)


def mix_kernel(below_ref, modes_ref, above_ref, weight_ref, table_ref, out_ref, held, mixed):
    lat_modes, deep, wide = weight_ref.shape
    ranks, levels, rows, _ = out_ref.shape
    chans = deep // 3
    band = wide // chans
    step = mixed.shape[1] // (lat_modes + 1)

    near = [below_ref[0].astype(F32)]
    near += [modes_ref[l].astype(F32) for l in range(levels)]
    near += [above_ref[0].astype(F32)]
    fill = [jnp.zeros((lat_modes, held.shape[0] * 128 - deep), F32)]
    for j in range(band):
        span = slice(j * chans, (j + 1) * chans)
        for l in range(levels):
            row = jnp.concatenate([near[l + d][:, span] for d in range(3)] + fill, axis=1)
            put(held, pl.ds(j * levels + l, lat_modes, stride=step), row)

    for k in range(lat_modes):
        at = slice(k * step, (k + 1) * step)
        lhs = jnp.concatenate([held[p, at, :] for p in range(held.shape[0])], axis=1)
        lhs = lhs[:, :deep].astype(BF)
        put(mixed, at, jnp.dot(lhs, weight_ref[k], preferred_element_type=F32))

    owner = lax.broadcasted_iota(jnp.int32, (lat_modes, wide), 1) // chans
    for l in range(levels):
        value = every(mixed, l, lat_modes, step)
        for j in range(1, band):
            value = jnp.where(owner == j, every(mixed, j * levels + l, lat_modes, step), value)
        value = value.astype(BF)
        back = jnp.dot(
            table_ref[...], jnp.concatenate([value, value], axis=0), preferred_element_type=F32
        )
        out_ref[:, l] = back.astype(BF).reshape(ranks, rows, wide)


def mix(below, modes, above, weight, table, ranks):
    levels, lat_modes, wide = modes.shape
    rows = table.shape[0] // ranks
    deep = weight.shape[1]
    step = (levels * wide * 3 // deep + 7) // 8 * 8
    return call(
        mix_kernel,
        (1,),
        [
            whole(below.shape),
            whole(modes.shape),
            whole(above.shape),
            whole(weight.shape),
            whole(table.shape),
        ],
        whole((ranks, levels, rows, wide)),
        jax.ShapeDtypeStruct((ranks, levels, rows, wide), BF),
        [lanes(lat_modes, step, (deep + 127) // 128 * 128), lanes(lat_modes, step, wide)],
        weight.size * 2 * levels,
        weight.size * 2,
    )(below, modes, above, weight, table)


def finish_kernel(
    batch_at, ahead, reach, back_ref, lon_ref, local_ref, bias_ref, into_ref, down_ref, loud_ref,
    field_ref, *rest
):
    (
        out_ref, held, coarse, act, hidden, into, act_scale, gate_scale, up_scale,
        taken, given, take_sem, give_sem,
    ) = rest[-13:]
    ranks, levels, rows, wide = back_ref.shape
    chans, cells = field_ref.shape[3:]
    band = wide // chans
    hid = down_ref.shape[1]
    total = levels * rows
    steps = total // ahead
    slots, kept = taken.shape[0], given.shape[0]
    tile = min(256, cells)
    spans = [slice(x, x + tile) for x in range(0, cells, tile)]

    def take(t):
        slot = lax.rem(t, slots)
        source = field_ref.at[batch_at, t // rows, lax.rem(t, rows)]
        return pltpu.make_async_copy(source, taken.at[slot], take_sem.at[slot])

    def give(t):
        slot = lax.rem(t, kept)
        target = out_ref.at[batch_at, t // rows, lax.rem(t, rows)]
        return pltpu.make_async_copy(given.at[slot], target, give_sem.at[slot])

    for t in range(min(slots - ahead, total)):
        take(jnp.int32(t)).start()

    for l in range(levels):
        put(
            held,
            slice(l * ranks * rows, (l + 1) * ranks * rows),
            back_ref[:, l].astype(F32).reshape(ranks * rows, wide),
        )

    def largest(x):
        return jnp.max(jnp.abs(x.astype(F32)), axis=(0, 1), keepdims=True)

    inverse = []
    for part in range(2):
        weight = into_ref[part * hid : (part + 1) * hid].astype(F32)
        scale, undo = power(largest(weight))
        inverse.append(undo)
        high, low = pieces(weight * scale)
        high, low = high.astype(F32), low.astype(F32)
        into[part * hid : (part + 1) * hid] = jnp.concatenate(
            [high, high, low, low], axis=1
        ).astype(F8)
    mixing = jnp.max(
        jnp.sum(jnp.abs(local_ref[...].astype(F32)), axis=1, keepdims=True), axis=0, keepdims=True
    )
    offset = largest(bias_ref[...])
    for l in range(levels):
        coarsest = functools.reduce(jnp.maximum, [jnp.abs(back_ref[r, l]) for r in range(ranks)])
        coarsest = jnp.max(coarsest.astype(F32), axis=1, keepdims=True)
        bound = 1.01 * (coarsest * reach + loud_ref[l] * mixing + offset)
        scale, undo = power(jnp.concatenate([bound] * (tile // 128), axis=1))
        at = slice(l * rows, (l + 1) * rows)
        act_scale[at] = 0.5 * scale
        gate_scale[at] = undo * inverse[0]
        up_scale[at] = undo * inverse[1]

    def prepare(u, t):
        t = jnp.minimum(t, total - 1)
        piece = every(held, (t // rows) * (ranks * rows) + lax.rem(t, rows), ranks, rows)
        stacked = jnp.concatenate(
            [piece[:, j * chans : (j + 1) * chans] for j in range(band)], axis=0
        )
        coarse[u] = jnp.concatenate([stacked.T.astype(BF), local_ref[...]], axis=1)

    def first(u, slot, span):
        both = jnp.concatenate([lon_ref[:, span], taken[slot, :, span]], axis=0)
        return jnp.dot(coarse[u], both, preferred_element_type=F32)

    def store_act(u, t, span, value):
        value = value + bias_ref[...]
        half = value * act_scale[pl.ds(t, 1), :]
        high, low = pieces((half + half * lax.erf(value * math.sqrt(0.5))).astype(BF))
        act[u, :chans, span] = high
        act[u, chans:, span] = low

    def last(u, t, slot, kept_at, span):
        down = jnp.dot(down_ref[...], hidden[u, :, span], preferred_element_type=F32)
        down = down * up_scale[pl.ds(t, 1), :]
        given[kept_at, :, span] = (taken[slot, :, span].astype(F32) + down).astype(BF)

    for u in range(ahead):
        prepare(u, jnp.int32(u))
    for u in range(ahead):
        take(jnp.int32(u)).wait()
        for span in spans:
            store_act(u, u, span, first(u, u, span))
    for u in range(ahead):
        prepare(u, jnp.int32(ahead + u))

    def one(step, carry):
        t = step * ahead

        @pl.when(step + 1 < steps)
        def _():
            for u in range(ahead):
                take(t + ahead + u).wait()

        @pl.when(t - ahead - kept >= 0)
        def _():
            for u in range(ahead):
                give(t - ahead - kept + u).wait()

        for u in range(ahead):
            before = t - ahead + u + slots * kept
            earlier = jnp.maximum(t - ahead + u, 0)
            later = jnp.minimum(t + ahead + u, total - 1)
            gate_undo = gate_scale[pl.ds(t + u, 1), :].astype(BF)
            for span in spans:
                ours = act[u, :, span]
                ours = jnp.concatenate([ours, ours], axis=0)
                both = jnp.dot(into[...], ours, preferred_element_type=F32)
                last(u, earlier, lax.rem(before, slots), lax.rem(before, kept), span)
                value = first(u, lax.rem(t + ahead + u, slots), span)
                half = both[:hid].astype(BF) * gate_undo
                hidden[u, :, span] = half * (1 + jnp.tanh(half)) * both[hid:].astype(BF)
                store_act(u, later, span, value)
            prepare(u, t + 2 * ahead + u)

        @pl.when(step > 0)
        def _():
            for u in range(ahead):
                give(t - ahead + u).start()

        @pl.when(t - ahead + slots < total)
        def _():
            for u in range(ahead):
                take(t - ahead + slots + u).start()

        return carry

    lax.fori_loop(0, steps, one, 0)
    for u in range(ahead):
        t = total - ahead + u
        if t >= kept:
            give(jnp.int32(t - kept)).wait()
        for span in spans:
            last(u, t, t % slots, t % kept, span)
        give(jnp.int32(t)).start()
    for t in range(max(total - kept, 0), total):
        give(jnp.int32(t)).wait()


def finish(field, back, lon_rows, local, bias, into, down, loud, reach, batch_at, earlier, ahead=2):
    batch, levels, rows, chans, cells = field.shape
    ranks, _, _, wide = back.shape
    modes = lon_rows.shape[0]
    slots, kept = 8 * ahead, 2 * ahead
    operands = [back, lon_rows, local, bias, into, down, loud, field]
    anywhere = pl.BlockSpec(memory_space=pl.ANY)
    in_specs = [whole(x.shape) for x in operands[:-1]] + [anywhere]
    kw = {}
    if earlier is not None:
        operands.append(earlier)
        in_specs.append(anywhere)
        kw["input_output_aliases"] = {8: 0}
    return call(
        functools.partial(finish_kernel, batch_at, ahead, reach),
        (1,),
        in_specs,
        anywhere,
        jax.ShapeDtypeStruct(field.shape, BF),
        [
            lanes(levels * ranks, rows, wide),
            pltpu.VMEM((ahead, chans, modes + chans), BF),
            pltpu.VMEM((ahead, 2 * chans, cells), F8),
            pltpu.VMEM((ahead, down.shape[1], cells), BF),
            pltpu.VMEM((2 * down.shape[1], 4 * chans), F8),
            *[pltpu.VMEM((levels * rows, min(256, cells)), F32)] * 3,
            pltpu.VMEM((slots, chans, cells), BF),
            pltpu.VMEM((kept, chans, cells), BF),
            pltpu.SemaphoreType.DMA((slots,)),
            pltpu.SemaphoreType.DMA((kept,)),
        ],
        2 * levels * rows * cells * chans * (modes + chans + 3 * down.shape[1]),
        levels * rows * chans * cells * 4,
        **kw,
    )(*operands)


def neighbours(modes, sides):
    if sides == 2:
        lower = lax.axis_index("lev") == 0
        got = lax.ppermute(
            jnp.where(lower, modes[-1:], modes[:1]), "lev", [(0, 1), (1, 0)]
        )
        none = jnp.zeros_like(got)
        return jnp.where(lower, none, got), jnp.where(lower, got, none)
    below = lax.ppermute(modes[-1:], "lev", [(i, i + 1) for i in range(sides - 1)])
    above = lax.ppermute(modes[:1], "lev", [(i + 1, i) for i in range(sides - 1)])
    return below, above


def body(field, spectral_weight, local_weight, local_bias, gate_weight, up_weight, down_weight):
    batch, levels, rows, chans, cells = field.shape
    ranks = lax.axis_size("rows")
    sides = lax.axis_size("lev")
    lat_modes = spectral_weight.shape[1]
    band = spectral_weight.shape[2]
    lon_modes = band * ranks
    lon_rows = cas_table(cells, lon_modes).astype(ml_dtypes.bfloat16).T
    lon_rows = lon_rows.reshape(ranks, band, cells).swapaxes(0, 1).reshape(lon_modes, cells)
    reach = float(np.abs(lon_rows.astype(np.float32)).sum(axis=0).max())
    lon_rows = jnp.asarray(np.ascontiguousarray(lon_rows))
    high, low = split(cas_table(rows * ranks, lat_modes))
    gather_table = jnp.asarray(np.concatenate([high.T, low.T], axis=0))
    spread_table = jnp.asarray(np.concatenate([high, low], axis=1))

    into = jnp.concatenate([gate_weight * BF(0.5), up_weight], axis=1).T
    down = down_weight.T
    local = local_weight.T
    bias = jnp.broadcast_to(local_bias[:, None], (chans, min(256, cells)))

    weight = arrange(spectral_weight)
    sent, loud = map(list, zip(*[forward(field, lon_rows, b, ranks) for b in range(batch)]))
    backs = []
    for b in range(batch):
        along = lax.all_to_all(sent[b], "rows", 0, 0, tiled=True)
        if b == 0:
            along, weight = lax.optimization_barrier((along, weight))
        modes = to_modes(gather_table, along)
        below, above = neighbours(modes, sides)
        back = mix(below, modes, above, weight, spread_table, ranks)
        backs.append(lax.all_to_all(back, "rows", 0, 0, tiled=True))
    result = None
    for b in range(batch):
        result = finish(
            field, backs[b], lon_rows, local, bias, into, down, loud[b], reach, b, result
        )
    return result


def solution(mesh):
    return jax.shard_map(
        body,
        mesh=mesh,
        in_specs=(
            P(None, "lev", "rows", None, None),
            P(None, None, "rows", None, None),
            P(),
            P(),
            P(),
            P(),
            P(),
        ),
        out_specs=P(None, "lev", "rows", None, None),
        check_vma=False,
    )
```
